128 devices in a mesh: section: 4 (over y_hi, core), block: 32 (over x, y_lo, z).
Axes of the slice: x: 4, y: 4 (y_hi: 2, y_lo: 2; y = y_hi * 2 + y_lo), z: 4, core: 2. Of those that a mesh axis runs over, the one named last changes fastest.
Arguments:
- inputs: bfloat16 [4, 16384, 128], P('section', 'block'), may hold values from -6 to 6
- cotangent: bfloat16 [4, 16384, 128], P('section', 'block'), may hold values from -6 to 6
- right_factor: bfloat16 [2, 4, 128, 128, 128], P(None, 'section', 'block'), may hold values from -0.5 to 0.5
- left_factor: bfloat16 [2, 4, 128, 128, 128], P(None, 'section', 'block'), may hold values from -0.5 to 0.5
Outputs:
- outputs: bfloat16 [4, 16384, 128], P('section', 'block')
- input_grad: bfloat16 [4, 16384, 128], P('section', 'block')
- right_grad: float32 [2, 4, 128, 128, 128], P(None, 'section', 'block')
- left_grad: float32 [2, 4, 128, 128, 128], P(None, 'section', 'block')
The draws below stay inside these ranges and needn't reach their ends.
All inputs are finite; a program needn't handle non-finite values.
Results may differ from the reference program's by a relative error of at most 0.04.
Values may be sent and summed in bfloat16 or wider, within the bound.
A program may use at most 64 MiB of HBM per device.

```python
import jax
import jax.numpy as jnp

D = 16384
BS = 128
NB = 128
MB = 128
LOOPS = 2
MICRO = 4
LAYERS = 8
N_SECTION = 4


def levels(key, shape, pieces, low, largest):
    gain = 1.0
    for position, blocks in pieces:
        steps = jax.random.uniform(jax.random.fold_in(jax.random.fold_in(key, 6), position), (blocks,), jnp.float32, low / len(pieces), largest / len(pieces))
        gain = gain * jnp.repeat(jnp.exp(steps), shape[position] // blocks).reshape((-1,) + (1,) * (len(shape) - 1 - position))
    return gain


def gaussian(rng, shape, deviation, most, pieces=(), held_as=jnp.bfloat16):
    gain = levels(rng, shape, pieces, -0.22, 0.18) if pieces else 1.0
    values = jax.random.normal(rng, shape, jnp.float32) * deviation * gain
    return jnp.minimum(jnp.maximum(values, -most), most).astype(held_as)


def setup_inputs(seed: int = 0) -> dict:
    streams_of = jax.random.split(jax.random.key(seed), 5)
    return {
        "inputs": gaussian(streams_of[0], (MICRO, D, MB), 1.0, 6.0, ((0, 4), (1, 32))),
        "cotangent": gaussian(streams_of[1], (MICRO, D, MB), 1.0, 6.0, ((0, 4), (1, 32))),
        "right_factor": gaussian(streams_of[2], (LOOPS, N_SECTION, NB, BS, BS), BS ** -0.5, 0.5, ((1, 4), (2, 32))),
        "left_factor": gaussian(streams_of[3], (LOOPS, N_SECTION, BS, NB, NB), NB ** -0.5, 0.5, ((1, 4), (2, 32))),
    }


def layer_forward(layer_input, right_block, left_block):
    acts = layer_input.reshape(NB, BS, -1).astype(jnp.float32)
    mixed = jnp.einsum('bjk,bjr->bkr', right_block.astype(jnp.float32), acts).astype(jnp.bfloat16)
    activated = jax.nn.silu(mixed.astype(jnp.float32)).astype(jnp.bfloat16)
    second = jnp.einsum('kbc,bkr->ckr', left_block.astype(jnp.float32), activated.astype(jnp.float32)).astype(jnp.bfloat16)
    result = (acts + second.astype(jnp.float32)).astype(jnp.bfloat16)
    return result.reshape(D, -1)


def layer_backward(layer_input, grad_out, right_block, left_block):
    acts = layer_input.reshape(NB, BS, -1).astype(jnp.float32)
    right_wide = right_block.astype(jnp.float32)
    left_wide = left_block.astype(jnp.float32)
    mixed = jnp.einsum('bjk,bjr->bkr', right_wide, acts).astype(jnp.bfloat16).astype(jnp.float32)
    activated = jax.nn.silu(mixed).astype(jnp.bfloat16).astype(jnp.float32)
    grad_wide = grad_out.reshape(NB, BS, -1).astype(jnp.float32)
    left_term = jnp.einsum('bkr,ckr->kbc', activated, grad_wide)
    grad_act = jnp.einsum('kbc,ckr->bkr', left_wide, grad_wide)
    sigmoid = jax.nn.sigmoid(mixed)
    grad_mixed = (grad_act * sigmoid * (1.0 + mixed * (1.0 - sigmoid))).astype(jnp.bfloat16).astype(jnp.float32)
    right_term = jnp.einsum('bjr,bkr->bjk', acts, grad_mixed)
    grad_in = (grad_wide + jnp.einsum('bjk,bkr->bjr', right_wide, grad_mixed)).astype(jnp.bfloat16)
    return grad_in.reshape(D, -1), right_term, left_term


def reference(inputs, cotangent, right_factor, left_factor):
    right_grad = jnp.zeros(right_factor.shape, jnp.float32)
    left_grad = jnp.zeros(left_factor.shape, jnp.float32)
    results = []
    grads_in = []
    for batch_slot in range(MICRO):
        current = inputs[batch_slot]
        stored = []
        for layer_index in range(LAYERS):
            loop_index = layer_index // N_SECTION
            section_index = layer_index % N_SECTION
            stored.append(current)
            current = layer_forward(current, right_factor[loop_index, section_index], left_factor[loop_index, section_index])
        results.append(current)
        grad_now = cotangent[batch_slot]
        for layer_index in range(LAYERS - 1, -1, -1):
            loop_index = layer_index // N_SECTION
            section_index = layer_index % N_SECTION
            grad_now, right_term, left_term = layer_backward(stored[layer_index], grad_now, right_factor[loop_index, section_index], left_factor[loop_index, section_index])
            right_grad = right_grad.at[loop_index, section_index].add(right_term)
            left_grad = left_grad.at[loop_index, section_index].add(left_term)
        grads_in.append(grad_now)
    return jnp.stack(results), jnp.stack(grads_in), right_grad, left_grad
```

```python
import functools

import jax
import jax.numpy as jnp
from jax import lax
from jax.experimental import pallas as pl
from jax.experimental.pallas import tpu as pltpu
from jax.sharding import PartitionSpec as P

MESH = pl.DeviceIdType.MESH
BF = jnp.bfloat16
F32 = jnp.float32
GROUP = 32
ROWS = 512
LANES = 128
LAYERS = 8
CHUNK = (GROUP, 16, LANES)


def dot(a, b):
    return jnp.dot(a, b, preferred_element_type=F32)


def dot_nt(a, b):
    return lax.dot_general(a, b, (((1,), (1,)), ((), ())), preferred_element_type=F32)


def kernel(
    x_ref, g_ref, r_ref, l_ref,
    out_x, out_g, out_r, out_l,
    wr, wl, land_x, land_g, hold_x, hold_g, back_x, back_g,
    rf, rb, lf, lb, m1, px, pxt, pa, pat,
    xs, us, acts, slope, usend, wsend, wrecv, gs, gc, dusend, durecv,
    held,
    wr_sem, wl_sem, w_send, land_sem, land_send, back_sem, back_send,
    a2a_send, a2a_recv, held_send, held_sem,
):
    section = lax.axis_index("section")
    block = lax.axis_index("block")
    yhi, core = section // 2, lax.rem(section, 2)
    xhi, low = block // 16, lax.rem(block, 16)
    place = core * 16 + low
    micro = 2 * yhi + xhi
    home = core == xhi
    away = core != xhi

    def remote(src, dst, ssem, rsem, device):
        return pltpu.make_async_remote_copy(
            src_ref=src, dst_ref=dst, send_sem=ssem, recv_sem=rsem,
            device_id={"section": device[0], "block": device[1]}, device_id_type=MESH)

    partner = (2 * yhi + xhi, core * 16 + low)

    barrier = pltpu.get_barrier_semaphore()
    greeted = []
    for i in range(1, GROUP):
        other = lax.rem(place + i, GROUP)
        greeted.append((yhi * 2 + other // 16, xhi * 16 + lax.rem(other, 16)))
    for dy in range(2):
        for dx in range(2):
            for dc in range(2):
                if dy or dx:
                    greeted.append((2 * lax.rem(yhi + dy, 2) + lax.rem(core + dc, 2),
                                    lax.rem(xhi + dx, 2) * 16 + low))
    for device in greeted:
        pl.semaphore_signal(barrier, inc=1, device_id={"section": device[0], "block": device[1]},
                            device_id_type=MESH)
    pl.semaphore_wait(barrier, len(greeted))

    def land(src, dst, i):
        return remote(src, dst, land_send.at[i], land_sem.at[i], partner)

    @pl.when(away)
    def _():
        land(x_ref, land_x, 0).start()

    def weight_copies(loop, act):
        layer = loop * 4 + section
        for kind, (src, dst, sem) in enumerate(((r_ref, wr, wr_sem), (l_ref, wl, wl_sem))):
            for i in range(4):
                dy, dx = i // 2, i % 2
                to_y, to_x = lax.rem(yhi + dy, 2), lax.rem(xhi + dx, 2)
                if i == 0:
                    @pl.when(home)
                    def _():
                        if act == "start":
                            pltpu.make_async_copy(src.at[loop], dst.at[layer], sem.at[layer]).start()

                    @pl.when(away)
                    def _():
                        copy = remote(src.at[loop], dst.at[layer], w_send.at[loop, kind, i],
                                      sem.at[layer], (2 * to_y + xhi, to_x * 16 + low))
                        if act == "start":
                            copy.start()
                        else:
                            copy.wait_send()
                else:
                    copy = remote(src.at[loop], dst.at[layer], w_send.at[loop, kind, i],
                                  sem.at[layer], (2 * to_y + xhi, to_x * 16 + low))
                    if act == "start":
                        copy.start()
                    else:
                        copy.wait_send()

    weight_copies(0, "start")

    @pl.when(away)
    def _():
        land(g_ref, land_g, 1).start()

    def one_hot(of_row, of_column):
        row = lax.broadcasted_iota(jnp.int32, (ROWS, ROWS), 0)
        column = lax.broadcasted_iota(jnp.int32, (ROWS, ROWS), 1)
        return jnp.where(of_row(row) == of_column(column), 1.0, 0.0).astype(BF)

    same = lambda v: v
    by_block = lambda v: ((v // 4) % 4) * 128 + (v // 16) * 4 + v % 4
    by_last = lambda v: (v % 4) * 128 + (v // 16) * 4 + (v // 4) % 4
    px[...] = one_hot(same, by_block)
    pxt[...] = one_hot(by_block, same)
    pa[...] = one_hot(same, by_last)
    pat[...] = one_hot(by_last, same)

    def expand(spread, spread_t, weights, forward, backward):
        for b in range(4):
            cols = pl.ds(b * 128, 128)
            m1[:, cols] = dot(spread_t[:, cols], weights[b]).astype(BF)
        for b in range(4):
            rows = pl.ds(b * 128, 128)
            backward[rows, :] = dot(m1[rows, :], spread[...]).astype(BF)
            forward[rows, :] = dot_nt(spread_t[rows, :], m1[...]).astype(BF)

    def wait_bytes(ref, sem):
        pltpu.make_async_copy(ref, ref, sem).wait()

    def expand_right(layer):
        wait_bytes(wr.at[layer], wr_sem.at[layer])
        expand(px, pxt, wr.at[layer], rf, rb.at[layer])

    def expand_left(layer):
        wait_bytes(wl.at[layer], wl_sem.at[layer])
        expand(pa, pat, wl.at[layer], lf, lb.at[layer])

    def exchange(kind, layer, src, dst):
        for i in range(1, GROUP):
            other = lax.rem(place + i, GROUP)
            remote(src.at[other], dst.at[place], a2a_send.at[kind, layer], a2a_recv.at[kind, layer],
                   (yhi * 2 + other // 16, xhi * 16 + lax.rem(other, 16))).start()
        dst[place] = src[place]

    def arrived(kind, layer, dst):
        wait_bytes(dst.at[pl.ds(0, GROUP - 1)], a2a_recv.at[kind, layer])

    def to_owner(kind, layer, src, act):
        loop, owner = layer // 4, lax.rem(layer, 4)
        mine = (owner == section) & home
        other = (owner != section) | away
        dst = held.at[loop, kind, micro]

        @pl.when(mine)
        def _():
            if act == "start":
                pltpu.make_async_copy(src, dst, held_sem.at[loop, kind]).start()

        @pl.when(other)
        def _():
            copy = remote(src, dst, held_send.at[kind, layer], held_sem.at[loop, kind],
                          (owner, core * 16 + low))
            if act == "start":
                copy.start()
            else:
                copy.wait_send()

    @pl.when(away)
    def _():
        wait_bytes(land_x, land_sem.at[0])
        xs[0] = dot(pxt[...], land_x[...]).astype(BF).reshape(CHUNK)

    @pl.when(home)
    def _():
        xs[0] = dot(pxt[...], x_ref[...]).astype(BF).reshape(CHUNK)

    expand_right(0)

    def forward_layer(layer, carry):
        x = xs[layer].reshape(ROWS, LANES)
        usend[layer] = dot(rf[...], x).astype(BF).reshape(CHUNK)
        exchange(0, layer, usend.at[layer], us.at[layer])

        @pl.when(layer == 0)
        def _():
            weight_copies(1, "start")

        to_owner(0, layer, xs.at[layer], "start")
        expand_left(layer)
        arrived(0, layer, us.at[layer])
        v = us[layer].reshape(ROWS, LANES).astype(F32)
        gate = 1.0 / (1.0 + jnp.exp(-v))
        act = (v * gate).astype(BF)
        wsend[layer] = dot(lf[...], act).astype(BF).reshape(CHUNK)
        exchange(1, layer, wsend.at[layer], wrecv.at[layer])
        acts[layer] = act.reshape(CHUNK)
        to_owner(1, layer, acts.at[layer], "start")
        slope[layer] = gate * (1.0 + v * (1.0 - gate))

        @pl.when(layer < LAYERS - 1)
        def _():
            expand_right(layer + 1)

        arrived(1, layer, wrecv.at[layer])
        xs[layer + 1] = (xs[layer].astype(F32) + wrecv[layer].astype(F32)).astype(BF)
        return carry

    lax.fori_loop(0, LAYERS, forward_layer, 0)

    @pl.when(away)
    def _():
        wait_bytes(land_g, land_sem.at[1])
        gs[LAYERS] = dot(pxt[...], land_g[...]).astype(BF).reshape(CHUNK)

    @pl.when(home)
    def _():
        gs[LAYERS] = dot(pxt[...], g_ref[...]).astype(BF).reshape(CHUNK)

    def give_back(i, src, dst, local):
        @pl.when(away)
        def _():
            remote(src, dst, back_send.at[i], back_sem.at[i], partner).start()

        @pl.when(home)
        def _():
            local[...] = src[...]

    def weight_grads(loop, spread, kind_a, kind_b, out):
        wait_bytes(held.at[loop, kind_a], held_sem.at[loop, kind_a])
        wait_bytes(held.at[loop, kind_b], held_sem.at[loop, kind_b])
        for m in range(4):
            a = dot(spread[...], held[loop, kind_a, m].reshape(ROWS, LANES)).astype(BF)
            b = dot(spread[...], held[loop, kind_b, m].reshape(ROWS, LANES)).astype(BF)
            for i in range(4):
                rows = slice(i * 128, i * 128 + 128)
                part = dot_nt(a[rows], b[rows])
                if m == 0:
                    out[loop, i] = part
                else:
                    out[loop, i] += part

    def backward_layer(step, carry):
        layer = LAYERS - 1 - step
        exchange(2, layer, gs.at[layer + 1], gc.at[layer])

        @pl.when(step == 0)
        def _():
            hold_x[...] = dot(px[...], xs[LAYERS].reshape(ROWS, LANES)).astype(BF)
            give_back(0, hold_x, back_x, out_x)

        @pl.when(step == 6)
        def _():
            weight_grads(1, px, 0, 3, out_r)

        arrived(2, layer, gc.at[layer])
        d_act = dot(lb[layer], gc[layer].reshape(ROWS, LANES))
        dusend[layer] = (d_act * slope[layer]).astype(BF).reshape(CHUNK)
        exchange(3, layer, dusend.at[layer], durecv.at[layer])
        to_owner(2, layer, gc.at[layer], "start")

        @pl.when(step == 5)
        def _():
            weight_grads(1, pa, 1, 2, out_l)

        arrived(3, layer, durecv.at[layer])
        to_owner(3, layer, durecv.at[layer], "start")
        branch = dot(rb[layer], durecv[layer].reshape(ROWS, LANES))
        gs[layer] = (gs[layer + 1].reshape(ROWS, LANES).astype(F32) + branch).astype(BF).reshape(CHUNK)
        return carry

    lax.fori_loop(0, LAYERS, backward_layer, 0)

    hold_g[...] = dot(px[...], gs[0].reshape(ROWS, LANES)).astype(BF)
    give_back(1, hold_g, back_g, out_g)
    weight_grads(0, pa, 1, 2, out_l)

    weight_copies(0, "wait")
    weight_copies(1, "wait")

    def sent(layer, carry):
        for kind, src in enumerate((xs, acts, gc, durecv)):
            to_owner(kind, layer, src.at[layer], "wait")
        for kind in range(4):
            wait_bytes(usend.at[layer, pl.ds(0, GROUP - 1)], a2a_send.at[kind, layer])
        return carry

    lax.fori_loop(0, LAYERS, sent, 0)

    @pl.when(away)
    def _():
        land(x_ref, land_x, 0).wait_send()
        land(g_ref, land_g, 1).wait_send()
        remote(hold_x, back_x, back_send.at[0], back_sem.at[0], partner).wait()
        out_x[...] = back_x[...]
        remote(hold_g, back_g, back_send.at[1], back_sem.at[1], partner).wait()
        out_g[...] = back_g[...]

    weight_grads(0, px, 0, 3, out_r)


def body(inputs, cotangent, right_factor, left_factor):
    vmem = pl.BlockSpec(memory_space=pltpu.VMEM)
    hbm = pl.BlockSpec(memory_space=pl.ANY)
    flat = (ROWS, LANES)
    blocks = (2, 4, 128, 128)
    buffer = lambda n: pltpu.VMEM((n,) + CHUNK, BF)
    dma = pltpu.SemaphoreType.DMA
    outs = pl.pallas_call(
        kernel,
        out_shape=[
            jax.ShapeDtypeStruct(flat, BF),
            jax.ShapeDtypeStruct(flat, BF),
            jax.ShapeDtypeStruct(blocks, F32),
            jax.ShapeDtypeStruct(blocks, F32),
        ],
        in_specs=[vmem, vmem, hbm, hbm],
        out_specs=[vmem] * 4,
        scratch_shapes=[
            pltpu.VMEM((LAYERS, 4, 128, 128), BF), pltpu.VMEM((LAYERS, 4, 128, 128), BF),
            pltpu.VMEM(flat, BF), pltpu.VMEM(flat, BF),
            pltpu.VMEM(flat, BF), pltpu.VMEM(flat, BF),
            pltpu.VMEM(flat, BF), pltpu.VMEM(flat, BF),
            pltpu.VMEM((ROWS, ROWS), BF), pltpu.VMEM((LAYERS, ROWS, ROWS), BF),
            pltpu.VMEM((ROWS, ROWS), BF), pltpu.VMEM((LAYERS, ROWS, ROWS), BF),
            *[pltpu.VMEM((ROWS, ROWS), BF)] * 5,
            buffer(LAYERS + 1), buffer(LAYERS), buffer(LAYERS),
            pltpu.VMEM((LAYERS, ROWS, LANES), F32),
            buffer(LAYERS), buffer(LAYERS), buffer(LAYERS),
            buffer(LAYERS + 1), buffer(LAYERS), buffer(LAYERS), buffer(LAYERS),
            pltpu.VMEM((2, 4, 4) + CHUNK, BF),
            dma((LAYERS,)), dma((LAYERS,)), dma((2, 2, 4)),
            dma((2,)), dma((2,)), dma((2,)), dma((2,)),
            dma((4, LAYERS)), dma((4, LAYERS)), dma((4, LAYERS)), dma((2, 4)),
        ],
        compiler_params=pltpu.CompilerParams(
            collective_id=0, has_side_effects=True, vmem_limit_bytes=56 * 1024 * 1024
        ),
        name="monarch_layers",
    )(
        inputs.reshape(flat),
        cotangent.reshape(flat),
        right_factor.reshape(blocks),
        left_factor.reshape(blocks),
    )
    out_x, out_g, out_r, out_l = outs
    return out_x[None], out_g[None], out_r[:, None], out_l[:, None]


def solution(mesh):
    acts = P("section", "block", None)
    factors = P(None, "section", "block", None, None)
    return jax.shard_map(
        body,
        mesh=mesh,
        in_specs=(acts, acts, factors, factors),
        out_specs=(acts, acts, factors, factors),
        check_vma=False,
    )
```

```python
import functools

import jax
import jax.numpy as jnp
from jax import lax
from jax.experimental import pallas as pl
from jax.experimental.pallas import tpu as pltpu
from jax.sharding import PartitionSpec as P

MESH = pl.DeviceIdType.MESH
BF = jnp.bfloat16
F32 = jnp.float32
GROUP = 32
ROWS = 512
LANES = 128
LAYERS = 8
CHUNK = (GROUP, 16, LANES)


def dot(a, b):
    return jnp.dot(a, b, preferred_element_type=F32)


def dot_nt(a, b):
    return lax.dot_general(a, b, (((1,), (1,)), ((), ())), preferred_element_type=F32)


def kernel(
    x_ref, g_ref, r_ref, l_ref,
    out_x, out_g, out_r, out_l,
    wr, wl, land_x, land_g, hold_x, hold_g, back_x, back_g,
    rf, rb, lf, lb, m1, px, pxt, pa, pat, total,
    xs, us, acts, slope, usend, wsend, wrecv, gs, gc, dusend, durecv,
    held,
    wr_sem, wl_sem, w_send, land_sem, land_send, back_sem, back_send,
    a2a_send, a2a_recv, held_send, held_sem,
):
    section = lax.axis_index("section")
    block = lax.axis_index("block")
    yhi, core = section // 2, lax.rem(section, 2)
    xhi, xat, ylo, z = block // 16, lax.rem(block // 8, 2), lax.rem(block // 4, 2), lax.rem(block, 4)
    home = core == xhi
    away = core != xhi
    xlo = lax.rem(xat + xhi + core, 2)
    owned = core * 16 + xlo * 8 + ylo * 4 + z
    place = xlo * 16 + ylo * 8 + core * 4 + z
    micro = 2 * yhi + xhi

    def remote(src, dst, ssem, rsem, device):
        return pltpu.make_async_remote_copy(
            src_ref=src, dst_ref=dst, send_sem=ssem, recv_sem=rsem,
            device_id={"section": device[0], "block": device[1]}, device_id_type=MESH)

    def member(mx, my, mcore, mz):
        at = lax.rem(mx + xhi + mcore, 2)
        return (yhi * 2 + mcore, xhi * 16 + at * 8 + my * 4 + mz)

    partner = (2 * yhi + xhi, owned)

    barrier = pltpu.get_barrier_semaphore()
    greeted = []
    for i in range(1, GROUP):
        greeted.append(member(lax.rem(xlo + i // 16, 2), lax.rem(ylo + (i // 8) % 2, 2),
                              lax.rem(core + (i // 4) % 2, 2), lax.rem(z + i % 4, 4)))
    for dy in range(2):
        for dx in range(2):
            for dc in range(2):
                if dy or dx:
                    greeted.append((2 * lax.rem(yhi + dy, 2) + lax.rem(core + dc, 2),
                                    lax.rem(xhi + dx, 2) * 16 + lax.rem(xat + dx, 2) * 8 + ylo * 4 + z))
    for device in greeted:
        pl.semaphore_signal(barrier, inc=1, device_id={"section": device[0], "block": device[1]},
                            device_id_type=MESH)
    pl.semaphore_wait(barrier, len(greeted))

    def land(src, dst, i):
        return remote(src, dst, land_send.at[i], land_sem.at[i], partner)

    @pl.when(away)
    def _():
        land(x_ref, land_x, 0).start()

    def weight_copies(loop, act, kinds=(0, 1)):
        layer = loop * 4 + section
        for kind in kinds:
            src, dst, sem = ((r_ref, wr, wr_sem), (l_ref, wl, wl_sem))[kind]
            for i in range(4):
                dy, dx = i // 2, i % 2
                to = (2 * lax.rem(yhi + dy, 2) + xhi,
                      lax.rem(xhi + dx, 2) * 16 + lax.rem(xat + dx, 2) * 8 + ylo * 4 + z)
                copy = functools.partial(remote, src.at[loop], dst.at[layer], w_send.at[loop, kind, i],
                                         sem.at[layer], to)
                move = lambda: copy().start() if act == "start" else copy().wait_send()
                if i == 0:
                    @pl.when(home)
                    def _():
                        if act == "start":
                            pltpu.make_async_copy(src.at[loop], dst.at[layer], sem.at[layer]).start()

                    @pl.when(away)
                    def _():
                        move()
                else:
                    move()

    weight_copies(0, "start")

    @pl.when(away)
    def _():
        land(g_ref, land_g, 1).start()

    def one_hot(of_row, of_column):
        row = lax.broadcasted_iota(jnp.int32, (ROWS, ROWS), 0)
        column = lax.broadcasted_iota(jnp.int32, (ROWS, ROWS), 1)
        return jnp.where(of_row(row) == of_column(column), 1.0, 0.0).astype(BF)

    same = lambda v: v
    quad = lambda v: (((v // 64) % 2) * 16 + (v // 128) * 4 + (v // 16) % 4) * 4
    by_block = lambda v: ((v // 4) % 4) * 128 + quad(v) + v % 4
    by_last = lambda v: (v % 4) * 128 + quad(v) + (v // 4) % 4
    px[...] = one_hot(same, by_block)
    pxt[...] = one_hot(by_block, same)
    pa[...] = one_hot(same, by_last)
    pat[...] = one_hot(by_last, same)

    def expand(spread, spread_t, weights, forward, backward):
        for b in range(4):
            cols = pl.ds(b * 128, 128)
            m1[:, cols] = dot(spread_t[:, cols], weights[b]).astype(BF)
        for b in range(4):
            rows = pl.ds(b * 128, 128)
            straight = dot(m1[rows, :], spread[...]).astype(BF)
            turned = dot_nt(spread_t[rows, :], m1[...]).astype(BF)
            for c in range(4):
                backward[c, b] = straight[:, c * 128 : c * 128 + 128]
                forward[c, b] = turned[:, c * 128 : c * 128 + 128]

    def wait_bytes(ref, sem):
        pltpu.make_async_copy(ref, ref, sem).wait()

    def expand_right(layer):
        wait_bytes(wr.at[layer], wr_sem.at[layer])
        expand(px, pxt, wr.at[layer], rf, rb.at[layer])

    def expand_left(layer):
        wait_bytes(wl.at[layer], wl_sem.at[layer])
        expand(pa, pat, wl.at[layer], lf, lb.at[layer])

    def chunk_of(relation):
        return lax.rem(xlo + relation // 2, 2) * 2 + lax.rem(ylo + relation % 2, 2)

    def rows_of(ref, chunk):
        return ref.at[pl.ds(chunk * 8, 8)]

    def send_chunk(kind, layer, relation, src, dst):
        chunk = chunk_of(relation)
        for i in (6, 2, 5, 7, 1, 3, 4, 0):
            if relation == 0 and i == 0:
                dst[place] = src[place]
                continue
            mcore, mz = lax.rem(core + i // 4, 2), lax.rem(z + i % 4, 4)
            other = chunk * 8 + mcore * 4 + mz
            remote(src.at[other], dst.at[place], a2a_send.at[kind, layer], a2a_recv.at[kind, layer, relation],
                   member(chunk // 2, lax.rem(chunk, 2), mcore, mz)).start()

    def arrived(kind, layer, relation, dst):
        wait_bytes(dst.at[pl.ds(0, 8 if relation else 7)], a2a_recv.at[kind, layer, relation])

    def stage(arrive, operand, weights, store, send):
        for n, relation in enumerate((0, 1, 2)):
            arrive(relation)
            chunk = chunk_of(relation)
            part = dot(weights[chunk].reshape(ROWS, 128), operand(chunk)).reshape(4, 128, LANES)
            if n == 0:
                total[...] = part
            else:
                total[...] += part
        arrive(3)
        last = chunk_of(3)
        value = operand(last)
        for relation in (3, 2, 1, 0):
            chunk = chunk_of(relation)
            store(chunk, total[chunk] + dot(weights[last, chunk], value))
            send(relation)

    def to_owner(kind, layer, src, act):
        loop, owner = layer // 4, lax.rem(layer, 4)
        mine = (owner == section) & home
        other = (owner != section) | away
        dst = held.at[loop, kind, micro]

        @pl.when(mine)
        def _():
            if act == "start":
                pltpu.make_async_copy(src, dst, held_sem.at[loop, kind]).start()

        @pl.when(other)
        def _():
            copy = remote(src, dst, held_send.at[kind, layer], held_sem.at[loop, kind], (owner, owned))
            if act == "start":
                copy.start()
            else:
                copy.wait_send()

    def flat(ref, chunk):
        return rows_of(ref, chunk)[...].reshape(128, LANES)

    def put(ref, chunk, value):
        rows_of(ref, chunk)[...] = value.reshape(8, 16, LANES)

    @pl.when(away)
    def _():
        wait_bytes(land_x, land_sem.at[0])
        xs[0] = dot(pxt[...], land_x[...]).astype(BF).reshape(CHUNK)

    @pl.when(home)
    def _():
        xs[0] = dot(pxt[...], x_ref[...]).astype(BF).reshape(CHUNK)

    expand_right(0)
    stage(
        lambda relation: None,
        lambda chunk: flat(xs.at[0], chunk),
        rf,
        lambda chunk, value: put(usend.at[0], chunk, value.astype(BF)),
        lambda relation: send_chunk(0, 0, relation, usend.at[0], us.at[0]),
    )
    weight_copies(1, "start", (0,))
    to_owner(0, 0, xs.at[0], "start")
    expand_left(0)

    def forward_layer(layer, carry):
        def activate(chunk):
            v = flat(us.at[layer], chunk).astype(F32)
            gate = 1.0 / (1.0 + jnp.exp(-v))
            act = (v * gate).astype(BF)
            put(acts.at[layer], chunk, act)
            slope[layer, chunk] = gate * (1.0 + v * (1.0 - gate))
            return act

        stage(
            lambda relation: arrived(0, layer, relation, us.at[layer]),
            activate,
            lf,
            lambda chunk, value: put(wsend.at[layer], chunk, value.astype(BF)),
            lambda relation: send_chunk(1, layer, relation, wsend.at[layer], wrecv.at[layer]),
        )

        @pl.when(layer == 0)
        def _():
            weight_copies(1, "start", (1,))

        to_owner(1, layer, acts.at[layer], "start")

        def step(chunk):
            new = flat(xs.at[layer], chunk).astype(F32) + flat(wrecv.at[layer], chunk).astype(F32)
            new = new.astype(BF)
            put(xs.at[layer + 1], chunk, new)
            return new

        @pl.when(layer < LAYERS - 1)
        def _():
            expand_right(layer + 1)
            stage(
                lambda relation: arrived(1, layer, relation, wrecv.at[layer]),
                step,
                rf,
                lambda chunk, value: put(usend.at[layer + 1], chunk, value.astype(BF)),
                lambda relation: send_chunk(0, layer + 1, relation, usend.at[layer + 1], us.at[layer + 1]),
            )
            to_owner(0, layer + 1, xs.at[layer + 1], "start")
            expand_left(layer + 1)

        @pl.when(layer == LAYERS - 1)
        def _():
            for relation in range(4):
                arrived(1, layer, relation, wrecv.at[layer])
                step(chunk_of(relation))

        return carry

    lax.fori_loop(0, LAYERS, forward_layer, 0)

    @pl.when(away)
    def _():
        wait_bytes(land_g, land_sem.at[1])
        gs[LAYERS] = dot(pxt[...], land_g[...]).astype(BF).reshape(CHUNK)

    @pl.when(home)
    def _():
        gs[LAYERS] = dot(pxt[...], g_ref[...]).astype(BF).reshape(CHUNK)

    for relation in (3, 2, 1, 0):
        send_chunk(2, LAYERS - 1, relation, gs.at[LAYERS], gc.at[LAYERS - 1])

    def give_back(i, src, dst, local):
        @pl.when(away)
        def _():
            remote(src, dst, back_send.at[i], back_sem.at[i], partner).start()

        @pl.when(home)
        def _():
            local[...] = src[...].astype(F32)

    hold_x[...] = dot(px[...], xs[LAYERS].reshape(ROWS, LANES)).astype(BF)
    give_back(0, hold_x, back_x, out_x)

    def weight_grads(loop, spread, kind_a, kind_b, out):
        wait_bytes(held.at[loop, kind_a], held_sem.at[loop, kind_a])
        wait_bytes(held.at[loop, kind_b], held_sem.at[loop, kind_b])
        for m in range(4):
            a = dot(spread[...], held[loop, kind_a, m].reshape(ROWS, LANES)).astype(BF)
            b = dot(spread[...], held[loop, kind_b, m].reshape(ROWS, LANES)).astype(BF)
            for i in range(4):
                rows = slice(i * 128, i * 128 + 128)
                part = dot_nt(a[rows], b[rows])
                if m == 0:
                    out[loop, i] = part
                else:
                    out[loop, i] += part

    def backward_layer(step, carry):
        layer = LAYERS - 1 - step

        def send_back(relation):
            @pl.when(layer > 0)
            def _():
                send_chunk(2, layer - 1, relation, gs.at[layer], gc.at[layer - 1])

        stage(
            lambda relation: arrived(2, layer, relation, gc.at[layer]),
            lambda chunk: flat(gc.at[layer], chunk),
            lb.at[layer],
            lambda chunk, value: put(dusend.at[layer], chunk, (value * slope[layer, chunk]).astype(BF)),
            lambda relation: send_chunk(3, layer, relation, dusend.at[layer], durecv.at[layer]),
        )
        to_owner(2, layer, gc.at[layer], "start")

        @pl.when(step == 5)
        def _():
            weight_grads(1, pa, 1, 2, out_l)

        @pl.when(step == 6)
        def _():
            weight_grads(1, px, 0, 3, out_r)

        stage(
            lambda relation: arrived(3, layer, relation, durecv.at[layer]),
            lambda chunk: flat(durecv.at[layer], chunk),
            rb.at[layer],
            lambda chunk, value: put(
                gs.at[layer], chunk, (flat(gs.at[layer + 1], chunk).astype(F32) + value).astype(BF)),
            send_back,
        )
        to_owner(3, layer, durecv.at[layer], "start")
        return carry

    lax.fori_loop(0, LAYERS, backward_layer, 0)

    hold_g[...] = dot(px[...], gs[0].reshape(ROWS, LANES)).astype(BF)
    give_back(1, hold_g, back_g, out_g)
    weight_grads(0, pa, 1, 2, out_l)

    weight_copies(0, "wait")
    weight_copies(1, "wait")

    def sent(layer, carry):
        for kind, src in enumerate((xs, acts, gc, durecv)):
            to_owner(kind, layer, src.at[layer], "wait")
        for kind in range(4):
            wait_bytes(usend.at[layer, pl.ds(0, GROUP - 1)], a2a_send.at[kind, layer])
        return carry

    lax.fori_loop(0, LAYERS, sent, 0)

    @pl.when(away)
    def _():
        land(x_ref, land_x, 0).wait_send()
        land(g_ref, land_g, 1).wait_send()
        remote(hold_x, back_x, back_send.at[0], back_sem.at[0], partner).wait()
        out_x[...] = back_x[...].astype(F32)
        remote(hold_g, back_g, back_send.at[1], back_sem.at[1], partner).wait()
        out_g[...] = back_g[...].astype(F32)

    weight_grads(0, px, 0, 3, out_r)


def body(inputs, cotangent, right_factor, left_factor):
    vmem = pl.BlockSpec(memory_space=pltpu.VMEM)
    hbm = pl.BlockSpec(memory_space=pl.ANY)
    flat = (ROWS, LANES)
    blocks = (2, 4, 128, 128)
    buffer = lambda n: pltpu.VMEM((n,) + CHUNK, BF)
    dma = pltpu.SemaphoreType.DMA
    outs = pl.pallas_call(
        kernel,
        out_shape=[
            jax.ShapeDtypeStruct(flat, F32),
            jax.ShapeDtypeStruct(flat, F32),
            jax.ShapeDtypeStruct(blocks, F32),
            jax.ShapeDtypeStruct(blocks, F32),
        ],
        in_specs=[vmem, vmem, hbm, hbm],
        out_specs=[vmem] * 4,
        scratch_shapes=[
            pltpu.VMEM((LAYERS, 4, 128, 128), BF), pltpu.VMEM((LAYERS, 4, 128, 128), BF),
            pltpu.VMEM(flat, BF), pltpu.VMEM(flat, BF),
            pltpu.VMEM(flat, BF), pltpu.VMEM(flat, BF),
            pltpu.VMEM(flat, BF), pltpu.VMEM(flat, BF),
            pltpu.VMEM((4, 4, 128, 128), BF), pltpu.VMEM((LAYERS, 4, 4, 128, 128), BF),
            pltpu.VMEM((4, 4, 128, 128), BF), pltpu.VMEM((LAYERS, 4, 4, 128, 128), BF),
            *[pltpu.VMEM((ROWS, ROWS), BF)] * 5,
            pltpu.VMEM((4, 128, LANES), F32),
            buffer(LAYERS + 1), buffer(LAYERS), buffer(LAYERS),
            pltpu.VMEM((LAYERS, 4, 128, LANES), F32),
            buffer(LAYERS), buffer(LAYERS), buffer(LAYERS),
            buffer(LAYERS + 1), buffer(LAYERS), buffer(LAYERS), buffer(LAYERS),
            pltpu.VMEM((2, 4, 4) + CHUNK, BF),
            dma((LAYERS,)), dma((LAYERS,)), dma((2, 2, 4)),
            dma((2,)), dma((2,)), dma((2,)), dma((2,)),
            dma((4, LAYERS)), dma((4, LAYERS, 4)), dma((4, LAYERS)), dma((2, 4)),
        ],
        compiler_params=pltpu.CompilerParams(
            collective_id=0, has_side_effects=True, vmem_limit_bytes=56 * 1024 * 1024
        ),
        name="monarch_layers",
    )(
        inputs.reshape(flat),
        cotangent.reshape(flat),
        right_factor.reshape(blocks),
        left_factor.reshape(blocks),
    )
    out_x, out_g, out_r, out_l = outs
    return out_x.astype(BF)[None], out_g.astype(BF)[None], out_r[:, None], out_l[:, None]


def solution(mesh):
    acts = P("section", "block", None)
    factors = P(None, "section", "block", None, None)
    return jax.shard_map(
        body,
        mesh=mesh,
        in_specs=(acts, acts, factors, factors),
        out_specs=(acts, acts, factors, factors),
        check_vma=False,
    )
```

```python
import functools

import jax
import jax.numpy as jnp
from jax import lax
from jax.experimental import pallas as pl
from jax.experimental.pallas import tpu as pltpu
from jax.sharding import PartitionSpec as P

MESH = pl.DeviceIdType.MESH
BF = jnp.bfloat16
F32 = jnp.float32
GROUP = 32
ROWS = 512
LANES = 128
LAYERS = 8
CHUNK = (GROUP, 16, LANES)


def dot(a, b):
    return jnp.dot(a, b, preferred_element_type=F32)


def sigmoid(v):
    return 0.5 + 0.5 * jnp.tanh(0.5 * v)


def dot_nt(a, b):
    return lax.dot_general(a, b, (((1,), (1,)), ((), ())), preferred_element_type=F32)


def kernel(
    x_ref, g_ref, r_ref, l_ref,
    out_x, out_g, out_r, out_l,
    wr, wl, land_x, land_g, hold_x, hold_g, back_x, back_g,
    rf, rb, lf, lb, m1, px, pxt, pa, pat,
    xs, us, acts, slope, usend, wsend, wrecv, gs, gc, dusend, durecv,
    grads, held,
    wr_sem, wl_sem, w_send, land_sem, land_send, back_sem, back_send,
    a2a_send, a2a_recv, held_send, held_sem,
):
    section = lax.axis_index("section")
    block = lax.axis_index("block")
    yhi, core = section // 2, lax.rem(section, 2)
    xhi, xat, ylo, z = block // 16, lax.rem(block // 8, 2), lax.rem(block // 4, 2), lax.rem(block, 4)
    home = core == xhi
    away = core != xhi
    xlo = lax.rem(xat + xhi + core, 2)
    owned = core * 16 + xlo * 8 + ylo * 4 + z
    place = xlo * 16 + ylo * 8 + core * 4 + z
    micro = 2 * yhi + xhi

    def remote(src, dst, ssem, rsem, device):
        return pltpu.make_async_remote_copy(
            src_ref=src, dst_ref=dst, send_sem=ssem, recv_sem=rsem,
            device_id={"section": device[0], "block": device[1]}, device_id_type=MESH)

    def member(mx, my, mcore, mz):
        at = lax.rem(mx + xhi + mcore, 2)
        return (yhi * 2 + mcore, xhi * 16 + at * 8 + my * 4 + mz)

    partner = (2 * yhi + xhi, owned)

    barrier = pltpu.get_barrier_semaphore()
    greeted = []
    for i in range(1, GROUP):
        greeted.append(member(lax.rem(xlo + i // 16, 2), lax.rem(ylo + (i // 8) % 2, 2),
                              lax.rem(core + (i // 4) % 2, 2), lax.rem(z + i % 4, 4)))
    for dy in range(2):
        for dx in range(2):
            for dc in range(2):
                if dy or dx:
                    greeted.append((2 * lax.rem(yhi + dy, 2) + lax.rem(core + dc, 2),
                                    lax.rem(xhi + dx, 2) * 16 + lax.rem(xat + dx, 2) * 8 + ylo * 4 + z))
    for device in greeted:
        pl.semaphore_signal(barrier, inc=1, device_id={"section": device[0], "block": device[1]},
                            device_id_type=MESH)
    pl.semaphore_wait(barrier, len(greeted))

    def land(src, dst, i):
        return remote(src, dst, land_send.at[i], land_sem.at[i], partner)

    @pl.when(away)
    def _():
        land(x_ref, land_x, 0).start()

    def weight_copies(loop, act, kinds=(0, 1)):
        layer = loop * 4 + section
        for kind in kinds:
            src, dst, sem = ((r_ref, wr, wr_sem), (l_ref, wl, wl_sem))[kind]
            for i in range(4):
                dy, dx = i // 2, i % 2
                to = (2 * lax.rem(yhi + dy, 2) + xhi,
                      lax.rem(xhi + dx, 2) * 16 + lax.rem(xat + dx, 2) * 8 + ylo * 4 + z)
                copy = functools.partial(remote, src.at[loop], dst.at[layer], w_send.at[loop, kind, i],
                                         sem.at[layer], to)
                move = lambda: copy().start() if act == "start" else copy().wait_send()
                if i == 0:
                    @pl.when(home)
                    def _():
                        if act == "start":
                            pltpu.make_async_copy(src.at[loop], dst.at[layer], sem.at[layer]).start()

                    @pl.when(away)
                    def _():
                        move()
                else:
                    move()

    weight_copies(0, "start", (0,))

    def one_hot(of_row, of_column):
        row = lax.broadcasted_iota(jnp.int32, (ROWS, ROWS), 0)
        column = lax.broadcasted_iota(jnp.int32, (ROWS, ROWS), 1)
        return jnp.where(of_row(row) == of_column(column), 1.0, 0.0).astype(BF)

    same = lambda v: v
    quad = lambda v: (((v // 64) % 2) * 16 + (v // 128) * 4 + (v // 16) % 4) * 4
    by_block = lambda v: ((v // 4) % 4) * 128 + quad(v) + v % 4
    by_last = lambda v: (v % 4) * 128 + quad(v) + (v // 4) % 4
    px[...] = one_hot(same, by_block)
    pxt[...] = one_hot(by_block, same)
    pa[...] = one_hot(same, by_last)
    pat[...] = one_hot(by_last, same)
    weight_copies(0, "start", (1,))

    @pl.when(away)
    def _():
        land(g_ref, land_g, 1).start()

    def expand(spread, spread_t, weights, forward, backward):
        for b in range(4):
            cols = pl.ds(b * 128, 128)
            m1[:, cols] = dot(spread_t[:, cols], weights[b]).astype(BF)
        for b in range(4):
            rows = pl.ds(b * 128, 128)
            backward[rows, :] = dot(m1[rows, :], spread[...]).astype(BF)
            forward[rows, :] = dot_nt(spread_t[rows, :], m1[...]).astype(BF)

    def wait_bytes(ref, sem):
        pltpu.make_async_copy(ref, ref, sem).wait()

    def expand_right(layer):
        wait_bytes(wr.at[layer], wr_sem.at[layer])
        expand(px, pxt, wr.at[layer], rf, rb.at[layer])

    def expand_left(layer):
        wait_bytes(wl.at[layer], wl_sem.at[layer])
        expand(pa, pat, wl.at[layer], lf, lb.at[layer])

    def chunk_of(relation):
        return lax.rem(xlo + relation // 2, 2) * 2 + lax.rem(ylo + relation % 2, 2)

    def rows_of(ref, chunk):
        return ref.at[pl.ds(chunk * 8, 8)]

    def send_chunk(kind, layer, relation, src, dst):
        chunk = chunk_of(relation)
        for i in (6, 2, 5, 7, 1, 3, 4, 0):
            if relation == 0 and i == 0:
                dst[place] = src[place]
                continue
            mcore, mz = lax.rem(core + i // 4, 2), lax.rem(z + i % 4, 4)
            other = chunk * 8 + mcore * 4 + mz
            remote(src.at[other], dst.at[place], a2a_send.at[kind, layer], a2a_recv.at[kind, layer, relation],
                   member(chunk // 2, lax.rem(chunk, 2), mcore, mz)).start()

    def arrived(kind, layer, relation, dst):
        wait_bytes(dst.at[pl.ds(0, 8 if relation else 7)], a2a_recv.at[kind, layer, relation])

    def stage(arrive, prepare, operand, weights, store, send):
        for relation in range(4):
            arrive(relation)
            if prepare is not None:
                prepare(chunk_of(relation))
        value = operand[...].reshape(ROWS, LANES)
        for pair in ((3, 2), (1, 0)):
            for relation in pair:
                chunk = chunk_of(relation)
                rows = pl.ds(pl.multiple_of(chunk * 128, 128), 128)
                store(chunk, dot(weights[rows, :], value))
            for relation in pair:
                send(relation)

    def to_owner(kind, layer, src, act):
        loop, owner = layer // 4, lax.rem(layer, 4)
        mine = (owner == section) & home
        other = (owner != section) | away
        dst = held.at[loop, kind, micro]

        @pl.when(mine)
        def _():
            if act == "start":
                pltpu.make_async_copy(src, dst, held_sem.at[loop, kind]).start()

        @pl.when(other)
        def _():
            copy = remote(src, dst, held_send.at[kind, layer], held_sem.at[loop, kind], (owner, owned))
            if act == "start":
                copy.start()
            else:
                copy.wait_send()

    def flat(ref, chunk):
        return rows_of(ref, chunk)[...].reshape(128, LANES)

    def put(ref, chunk, value):
        rows_of(ref, chunk)[...] = value.reshape(8, 16, LANES)

    @pl.when(away)
    def _():
        wait_bytes(land_x, land_sem.at[0])
        xs[0] = dot(pxt[...], land_x[...]).astype(BF).reshape(CHUNK)

    @pl.when(home)
    def _():
        xs[0] = dot(pxt[...], x_ref[...]).astype(BF).reshape(CHUNK)

    expand_right(0)
    stage(
        lambda relation: None,
        None,
        xs.at[0],
        rf,
        lambda chunk, value: put(usend.at[0], chunk, value.astype(BF)),
        lambda relation: send_chunk(0, 0, relation, usend.at[0], us.at[0]),
    )
    weight_copies(1, "start", (0,))
    expand_left(0)

    def forward_layer(layer, carry):
        def activate(chunk):
            v = flat(us.at[layer], chunk).astype(F32)
            put(acts.at[layer], chunk, (v * sigmoid(v)).astype(BF))

        stage(
            lambda relation: arrived(0, layer, relation, us.at[layer]),
            activate,
            acts.at[layer],
            lf,
            lambda chunk, value: put(wsend.at[layer], chunk, value.astype(BF)),
            lambda relation: send_chunk(1, layer, relation, wsend.at[layer], wrecv.at[layer]),
        )

        @pl.when(layer == 0)
        def _():
            weight_copies(1, "start", (1,))

        for chunk in range(4):
            v = flat(us.at[layer], chunk).astype(F32)
            gate = sigmoid(v)
            slope[layer, chunk] = gate * (1.0 + v * (1.0 - gate))

        def step(chunk):
            new = flat(xs.at[layer], chunk).astype(F32) + flat(wrecv.at[layer], chunk).astype(F32)
            put(xs.at[layer + 1], chunk, new.astype(BF))

        @pl.when(layer < LAYERS - 1)
        def _():
            expand_right(layer + 1)
            stage(
                lambda relation: arrived(1, layer, relation, wrecv.at[layer]),
                step,
                xs.at[layer + 1],
                rf,
                lambda chunk, value: put(usend.at[layer + 1], chunk, value.astype(BF)),
                lambda relation: send_chunk(0, layer + 1, relation, usend.at[layer + 1], us.at[layer + 1]),
            )
            expand_left(layer + 1)

        @pl.when(layer == LAYERS - 1)
        def _():
            for relation in range(4):
                arrived(1, layer, relation, wrecv.at[layer])
                step(chunk_of(relation))

        return carry

    lax.fori_loop(0, LAYERS, forward_layer, 0)

    @pl.when(away)
    def _():
        wait_bytes(land_g, land_sem.at[1])
        gs[LAYERS] = dot(pxt[...], land_g[...]).astype(BF).reshape(CHUNK)

    @pl.when(home)
    def _():
        gs[LAYERS] = dot(pxt[...], g_ref[...]).astype(BF).reshape(CHUNK)

    for relation in (3, 2, 1, 0):
        send_chunk(2, LAYERS - 1, relation, gs.at[LAYERS], gc.at[LAYERS - 1])

    def give_back(i, src, dst, local):
        @pl.when(away)
        def _():
            remote(src, dst, back_send.at[i], back_sem.at[i], partner).start()

        @pl.when(home)
        def _():
            local[...] = src[...].astype(F32)

    hold_x[...] = dot(px[...], xs[LAYERS].reshape(ROWS, LANES)).astype(BF)
    give_back(0, hold_x, back_x, out_x)

    def weight_grad(kind, layer, spread, left, right):
        a = dot(spread[...], left[layer].reshape(ROWS, LANES)).astype(BF)
        b = dot(spread[...], right[layer].reshape(ROWS, LANES)).astype(BF)
        for i in range(4):
            rows = slice(i * 128, i * 128 + 128)
            grads[kind, layer, i] = dot_nt(a[rows], b[rows]).astype(BF)
        to_owner(kind, layer, grads.at[kind, layer], "start")

    def add_up(loop, kind, out):
        wait_bytes(held.at[loop, kind], held_sem.at[loop, kind])
        for i in range(4):
            terms = [held[loop, kind, m, i].astype(F32) for m in range(4)]
            out[loop, i] = (terms[0] + terms[1]) + (terms[2] + terms[3])

    def backward_layer(step, carry):
        layer = LAYERS - 1 - step

        def send_back(relation):
            @pl.when(layer > 0)
            def _():
                send_chunk(2, layer - 1, relation, gs.at[layer], gc.at[layer - 1])

        stage(
            lambda relation: arrived(2, layer, relation, gc.at[layer]),
            None,
            gc.at[layer],
            lb.at[layer],
            lambda chunk, value: put(dusend.at[layer], chunk, (value * slope[layer, chunk]).astype(BF)),
            lambda relation: send_chunk(3, layer, relation, dusend.at[layer], durecv.at[layer]),
        )
        weight_grad(1, layer, pa, acts, gc)

        @pl.when(step == 5)
        def _():
            add_up(1, 0, out_r)

        @pl.when(step == 6)
        def _():
            add_up(1, 1, out_l)

        stage(
            lambda relation: arrived(3, layer, relation, durecv.at[layer]),
            None,
            durecv.at[layer],
            rb.at[layer],
            lambda chunk, value: put(
                gs.at[layer], chunk, (flat(gs.at[layer + 1], chunk).astype(F32) + value).astype(BF)),
            send_back,
        )
        weight_grad(0, layer, px, xs, durecv)
        return carry

    lax.fori_loop(0, LAYERS, backward_layer, 0)

    hold_g[...] = dot(px[...], gs[0].reshape(ROWS, LANES)).astype(BF)
    give_back(1, hold_g, back_g, out_g)
    add_up(0, 1, out_l)

    weight_copies(0, "wait")
    weight_copies(1, "wait")

    def sent(layer, carry):
        for kind in range(2):
            to_owner(kind, layer, grads.at[kind, layer], "wait")
        for kind in range(4):
            wait_bytes(usend.at[layer, pl.ds(0, GROUP - 1)], a2a_send.at[kind, layer])
        return carry

    lax.fori_loop(0, LAYERS, sent, 0)

    @pl.when(away)
    def _():
        land(x_ref, land_x, 0).wait_send()
        land(g_ref, land_g, 1).wait_send()
        remote(hold_x, back_x, back_send.at[0], back_sem.at[0], partner).wait()
        out_x[...] = back_x[...].astype(F32)
        remote(hold_g, back_g, back_send.at[1], back_sem.at[1], partner).wait()
        out_g[...] = back_g[...].astype(F32)

    add_up(0, 0, out_r)


def body(inputs, cotangent, right_factor, left_factor):
    vmem = pl.BlockSpec(memory_space=pltpu.VMEM)
    hbm = pl.BlockSpec(memory_space=pl.ANY)
    flat = (ROWS, LANES)
    blocks = (2, 4, 128, 128)
    buffer = lambda n: pltpu.VMEM((n,) + CHUNK, BF)
    dma = pltpu.SemaphoreType.DMA
    outs = pl.pallas_call(
        kernel,
        out_shape=[
            jax.ShapeDtypeStruct(flat, F32),
            jax.ShapeDtypeStruct(flat, F32),
            jax.ShapeDtypeStruct(blocks, F32),
            jax.ShapeDtypeStruct(blocks, F32),
        ],
        in_specs=[vmem, vmem, hbm, hbm],
        out_specs=[vmem] * 4,
        scratch_shapes=[
            pltpu.VMEM((LAYERS, 4, 128, 128), BF), pltpu.VMEM((LAYERS, 4, 128, 128), BF),
            pltpu.VMEM(flat, BF), pltpu.VMEM(flat, BF),
            pltpu.VMEM(flat, BF), pltpu.VMEM(flat, BF),
            pltpu.VMEM(flat, BF), pltpu.VMEM(flat, BF),
            pltpu.VMEM((ROWS, ROWS), BF), pltpu.VMEM((LAYERS, ROWS, ROWS), BF),
            pltpu.VMEM((ROWS, ROWS), BF), pltpu.VMEM((LAYERS, ROWS, ROWS), BF),
            *[pltpu.VMEM((ROWS, ROWS), BF)] * 5,
            buffer(LAYERS + 1), buffer(LAYERS), buffer(LAYERS),
            pltpu.VMEM((LAYERS, 4, 128, LANES), F32),
            buffer(LAYERS), buffer(LAYERS), buffer(LAYERS),
            buffer(LAYERS + 1), buffer(LAYERS), buffer(LAYERS), buffer(LAYERS),
            pltpu.VMEM((2, LAYERS, 4, 128, 128), BF), pltpu.VMEM((2, 2, 4, 4, 128, 128), BF),
            dma((LAYERS,)), dma((LAYERS,)), dma((2, 2, 4)),
            dma((2,)), dma((2,)), dma((2,)), dma((2,)),
            dma((4, LAYERS)), dma((4, LAYERS, 4)), dma((2, LAYERS)), dma((2, 2)),
        ],
        compiler_params=pltpu.CompilerParams(
            collective_id=0, has_side_effects=True, vmem_limit_bytes=56 * 1024 * 1024
        ),
        name="monarch_layers",
    )(
        inputs.reshape(flat),
        cotangent.reshape(flat),
        right_factor.reshape(blocks),
        left_factor.reshape(blocks),
    )
    out_x, out_g, out_r, out_l = outs
    return out_x.astype(BF)[None], out_g.astype(BF)[None], out_r[:, None], out_l[:, None]


def solution(mesh):
    acts = P("section", "block", None)
    factors = P(None, "section", "block", None, None)
    return jax.shard_map(
        body,
        mesh=mesh,
        in_specs=(acts, acts, factors, factors),
        out_specs=(acts, acts, factors, factors),
        check_vma=False,
    )
```

```python
import functools

import jax
import jax.numpy as jnp
from jax import lax
from jax.experimental import pallas as pl
from jax.experimental.pallas import tpu as pltpu
from jax.sharding import PartitionSpec as P

MESH = pl.DeviceIdType.MESH
BF = jnp.bfloat16
F32 = jnp.float32
GROUP = 32
ROWS = 512
LANES = 128
LAYERS = 8
CHUNK = (GROUP, 16, LANES)


def dot(a, b):
    return jnp.dot(a, b, preferred_element_type=F32)


def sigmoid(v):
    return 0.5 + 0.5 * jnp.tanh(0.5 * v)


def dot_tn(a, b):
    return lax.dot_general(a, b, (((0,), (0,)), ((), ())), preferred_element_type=F32)


def dot_nt(a, b):
    return lax.dot_general(a, b, (((1,), (1,)), ((), ())), preferred_element_type=F32)


def kernel(
    x_ref, g_ref, r_ref, l_ref,
    out_x, out_g, out_r, out_l,
    wr, wl, land_x, land_g, hold_x, hold_g, back_x, back_g,
    rf, rb, lf, lb, m1, px, pxt, pa, pat,
    xs, us, acts, slope, usend, wsend, wrecv, gs, gc, dusend, durecv,
    grads, held,
    wr_sem, wl_sem, w_send, land_sem, land_send, back_sem, back_send,
    a2a_send, a2a_recv, held_send, held_sem,
):
    section = lax.axis_index("section")
    block = lax.axis_index("block")
    yhi, core = section // 2, lax.rem(section, 2)
    xhi, xat, ylo, z = block // 16, lax.rem(block // 8, 2), lax.rem(block // 4, 2), lax.rem(block, 4)
    home = core == xhi
    away = core != xhi
    xlo = lax.rem(xat + xhi + core, 2)
    owned = core * 16 + xlo * 8 + ylo * 4 + z
    place = xlo * 16 + ylo * 8 + core * 4 + z
    micro = 2 * yhi + xhi

    def remote(src, dst, ssem, rsem, device):
        return pltpu.make_async_remote_copy(
            src_ref=src, dst_ref=dst, send_sem=ssem, recv_sem=rsem,
            device_id={"section": device[0], "block": device[1]}, device_id_type=MESH)

    def member(mx, my, mcore, mz):
        at = lax.rem(mx + xhi + mcore, 2)
        return (yhi * 2 + mcore, xhi * 16 + at * 8 + my * 4 + mz)

    partner = (2 * yhi + xhi, owned)

    barrier = pltpu.get_barrier_semaphore()
    greeted = []
    for i in range(1, GROUP):
        greeted.append(member(lax.rem(xlo + i // 16, 2), lax.rem(ylo + (i // 8) % 2, 2),
                              lax.rem(core + (i // 4) % 2, 2), lax.rem(z + i % 4, 4)))
    for dy in range(2):
        for dx in range(2):
            for dc in range(2):
                if dy or dx:
                    greeted.append((2 * lax.rem(yhi + dy, 2) + lax.rem(core + dc, 2),
                                    lax.rem(xhi + dx, 2) * 16 + lax.rem(xat + dx, 2) * 8 + ylo * 4 + z))
    for device in greeted:
        pl.semaphore_signal(barrier, inc=1, device_id={"section": device[0], "block": device[1]},
                            device_id_type=MESH)
    pl.semaphore_wait(barrier, len(greeted))

    def land(src, dst, i):
        return remote(src, dst, land_send.at[i], land_sem.at[i], partner)

    @pl.when(away)
    def _():
        land(x_ref, land_x, 0).start()

    def weight_copies(loop, act, kinds=(0, 1)):
        layer = loop * 4 + section
        for kind in kinds:
            src, dst, sem = ((r_ref, wr, wr_sem), (l_ref, wl, wl_sem))[kind]
            for i in range(4):
                dy, dx = i // 2, i % 2
                to = (2 * lax.rem(yhi + dy, 2) + xhi,
                      lax.rem(xhi + dx, 2) * 16 + lax.rem(xat + dx, 2) * 8 + ylo * 4 + z)
                copy = functools.partial(remote, src.at[loop], dst.at[layer], w_send.at[loop, kind, i],
                                         sem.at[layer], to)
                move = lambda: copy().start() if act == "start" else copy().wait_send()
                if i == 0:
                    @pl.when(home)
                    def _():
                        if act == "start":
                            pltpu.make_async_copy(src.at[loop], dst.at[layer], sem.at[layer]).start()

                    @pl.when(away)
                    def _():
                        move()
                else:
                    move()

    @pl.when(section == 0)
    def _():
        weight_copies(0, "start", (0,))

    def one_hot(of_row, of_column):
        row = lax.broadcasted_iota(jnp.int32, (ROWS, ROWS), 0)
        column = lax.broadcasted_iota(jnp.int32, (ROWS, ROWS), 1)
        return jnp.where(of_row(row) == of_column(column), 1.0, 0.0).astype(BF)

    same = lambda v: v
    quad = lambda v: (((v // 64) % 2) * 16 + (v // 128) * 4 + (v // 16) % 4) * 4
    by_block = lambda v: ((v // 4) % 4) * 128 + quad(v) + v % 4
    by_last = lambda v: (v % 4) * 128 + quad(v) + (v // 4) % 4
    px[...] = one_hot(same, by_block)
    pxt[...] = one_hot(by_block, same)
    pa[...] = one_hot(same, by_last)
    pat[...] = one_hot(by_last, same)

    @pl.when(section != 0)
    def _():
        weight_copies(0, "start", (0,))

    weight_copies(0, "start", (1,))

    @pl.when(away)
    def _():
        land(g_ref, land_g, 1).start()

    def expand(spread, spread_t, weights, forward, backward):
        for b in range(4):
            cols = pl.ds(b * 128, 128)
            m1[:, cols] = dot(spread_t[:, cols], weights[b]).astype(BF)
        for b in range(4):
            rows = pl.ds(b * 128, 128)
            backward[rows, :] = dot(m1[rows, :], spread[...]).astype(BF)
            forward[rows, :] = dot_nt(spread_t[rows, :], m1[...]).astype(BF)

    def wait_bytes(ref, sem):
        pltpu.make_async_copy(ref, ref, sem).wait()

    def expand_right(layer):
        wait_bytes(wr.at[layer], wr_sem.at[layer])
        expand(px, pxt, wr.at[layer], rf, rb.at[layer])

    def expand_left(layer):
        wait_bytes(wl.at[layer], wl_sem.at[layer])
        expand(pa, pat, wl.at[layer], lf, lb.at[layer])

    def chunk_of(relation):
        return lax.rem(xlo + relation // 2, 2) * 2 + lax.rem(ylo + relation % 2, 2)

    def rows_of(ref, chunk):
        return ref.at[pl.ds(chunk * 8, 8)]

    def send_chunk(kind, layer, relation, src, dst):
        chunk = chunk_of(relation)
        for i in (6, 2, 5, 7, 1, 3, 4, 0):
            if relation == 0 and i == 0:
                dst[place] = src[place]
                continue
            mcore, mz = lax.rem(core + i // 4, 2), lax.rem(z + i % 4, 4)
            other = chunk * 8 + mcore * 4 + mz
            remote(src.at[other], dst.at[place], a2a_send.at[kind, layer], a2a_recv.at[kind, layer, relation],
                   member(chunk // 2, lax.rem(chunk, 2), mcore, mz)).start()

    def arrived(kind, layer, relation, dst):
        wait_bytes(dst.at[pl.ds(0, 8 if relation else 7)], a2a_recv.at[kind, layer, relation])

    def stage(arrive, prepare, operand, weights, store, send):
        for relation in range(4):
            arrive(relation)
            if prepare is not None:
                prepare(chunk_of(relation))
        value = operand[...].reshape(ROWS, LANES)
        for pair in ((3, 2), (1, 0)):
            for relation in pair:
                chunk = chunk_of(relation)
                rows = pl.ds(pl.multiple_of(chunk * 128, 128), 128)
                store(chunk, dot(weights[rows, :], value))
            for relation in pair:
                send(relation)

    def to_owner(kind, layer, src, act):
        loop, owner = layer // 4, lax.rem(layer, 4)
        mine = (owner == section) & home
        other = (owner != section) | away
        dst = held.at[loop, kind, micro]

        @pl.when(mine)
        def _():
            if act == "start":
                pltpu.make_async_copy(src, dst, held_sem.at[loop, kind]).start()

        @pl.when(other)
        def _():
            copy = remote(src, dst, held_send.at[kind, layer], held_sem.at[loop, kind], (owner, owned))
            if act == "start":
                copy.start()
            else:
                copy.wait_send()

    def flat(ref, chunk):
        return rows_of(ref, chunk)[...].reshape(128, LANES)

    def put(ref, chunk, value):
        rows_of(ref, chunk)[...] = value.reshape(8, 16, LANES)

    @pl.when(away)
    def _():
        wait_bytes(land_x, land_sem.at[0])
        hold_x[...] = land_x[...]

    @pl.when(home)
    def _():
        hold_x[...] = x_ref[...]

    xs[0] = dot(pxt[...], hold_x[...]).astype(BF).reshape(CHUNK)
    wait_bytes(wr.at[0], wr_sem.at[0])
    for b in range(4):
        rows = pl.ds(b * 128, 128)
        hold_g[rows, :] = dot_tn(wr[0, b], hold_x[rows, :]).astype(BF)
    stage(
        lambda relation: None,
        None,
        hold_g,
        pxt,
        lambda chunk, value: put(usend.at[0], chunk, value.astype(BF)),
        lambda relation: send_chunk(0, 0, relation, usend.at[0], us.at[0]),
    )
    weight_copies(1, "start", (0,))
    expand_left(0)

    def forward_layer(layer, carry):
        def activate(chunk):
            v = flat(us.at[layer], chunk).astype(F32)
            put(acts.at[layer], chunk, (v * sigmoid(v)).astype(BF))

        stage(
            lambda relation: arrived(0, layer, relation, us.at[layer]),
            activate,
            acts.at[layer],
            lf,
            lambda chunk, value: put(wsend.at[layer], chunk, value.astype(BF)),
            lambda relation: send_chunk(1, layer, relation, wsend.at[layer], wrecv.at[layer]),
        )

        @pl.when(layer == 0)
        def _():
            weight_copies(1, "start", (1,))

        for chunk in range(4):
            v = flat(us.at[layer], chunk).astype(F32)
            gate = sigmoid(v)
            slope[layer, chunk] = gate * (1.0 + v * (1.0 - gate))

        def step(chunk):
            new = flat(xs.at[layer], chunk).astype(F32) + flat(wrecv.at[layer], chunk).astype(F32)
            put(xs.at[layer + 1], chunk, new.astype(BF))

        @pl.when(layer < LAYERS - 1)
        def _():
            expand_right(layer + 1)
            stage(
                lambda relation: arrived(1, layer, relation, wrecv.at[layer]),
                step,
                xs.at[layer + 1],
                rf,
                lambda chunk, value: put(usend.at[layer + 1], chunk, value.astype(BF)),
                lambda relation: send_chunk(0, layer + 1, relation, usend.at[layer + 1], us.at[layer + 1]),
            )
            expand_left(layer + 1)

        @pl.when(layer == LAYERS - 1)
        def _():
            expand(px, pxt, wr.at[0], rf, rb.at[0])
            for relation in range(4):
                arrived(1, layer, relation, wrecv.at[layer])
                step(chunk_of(relation))

        return carry

    lax.fori_loop(0, LAYERS, forward_layer, 0)

    @pl.when(away)
    def _():
        wait_bytes(land_g, land_sem.at[1])
        gs[LAYERS] = dot(pxt[...], land_g[...]).astype(BF).reshape(CHUNK)

    @pl.when(home)
    def _():
        gs[LAYERS] = dot(pxt[...], g_ref[...]).astype(BF).reshape(CHUNK)

    for relation in (3, 2, 1, 0):
        send_chunk(2, LAYERS - 1, relation, gs.at[LAYERS], gc.at[LAYERS - 1])

    def give_back(i, src, dst, local):
        @pl.when(away)
        def _():
            remote(src, dst, back_send.at[i], back_sem.at[i], partner).start()

        @pl.when(home)
        def _():
            local[...] = src[...]

    hold_x[...] = dot(px[...], xs[LAYERS].reshape(ROWS, LANES)).astype(BF)
    give_back(0, hold_x, back_x, out_x)

    def weight_grad(kind, layer, spread, left, right):
        a = dot(spread[...], left[layer].reshape(ROWS, LANES)).astype(BF)
        b = dot(spread[...], right[layer].reshape(ROWS, LANES)).astype(BF)
        for i in range(4):
            rows = slice(i * 128, i * 128 + 128)
            grads[kind, layer, i] = dot_nt(a[rows], b[rows]).astype(BF)
        to_owner(kind, layer, grads.at[kind, layer], "start")

    def add_up(loop, kind, out):
        wait_bytes(held.at[loop, kind], held_sem.at[loop, kind])
        for i in range(4):
            terms = [held[loop, kind, m, i].astype(F32) for m in range(4)]
            out[loop, i] = (terms[0] + terms[1]) + (terms[2] + terms[3])

    def backward_layer(step, carry):
        layer = LAYERS - 1 - step

        def send_back(relation):
            @pl.when(layer > 0)
            def _():
                send_chunk(2, layer - 1, relation, gs.at[layer], gc.at[layer - 1])

        stage(
            lambda relation: arrived(2, layer, relation, gc.at[layer]),
            None,
            gc.at[layer],
            lb.at[layer],
            lambda chunk, value: put(dusend.at[layer], chunk, (value * slope[layer, chunk]).astype(BF)),
            lambda relation: send_chunk(3, layer, relation, dusend.at[layer], durecv.at[layer]),
        )
        weight_grad(1, layer, pa, acts, gc)

        @pl.when(step == 5)
        def _():
            add_up(1, 0, out_r)

        @pl.when(step == 6)
        def _():
            add_up(1, 1, out_l)

        for relation in range(4):
            arrived(3, layer, relation, durecv.at[layer])

        @pl.when(layer == 0)
        def _():
            weight_grad(0, layer, px, xs, durecv)

        stage(
            lambda relation: None,
            None,
            durecv.at[layer],
            rb.at[layer],
            lambda chunk, value: put(
                gs.at[layer], chunk, (flat(gs.at[layer + 1], chunk).astype(F32) + value).astype(BF)),
            send_back,
        )

        @pl.when(layer > 0)
        def _():
            weight_grad(0, layer, px, xs, durecv)

        return carry

    lax.fori_loop(0, LAYERS, backward_layer, 0)

    hold_g[...] = dot(px[...], gs[0].reshape(ROWS, LANES)).astype(BF)
    give_back(1, hold_g, back_g, out_g)
    add_up(0, 1, out_l)

    weight_copies(0, "wait")
    weight_copies(1, "wait")

    def sent(layer, carry):
        for kind in range(2):
            to_owner(kind, layer, grads.at[kind, layer], "wait")
        for kind in range(4):
            wait_bytes(usend.at[layer, pl.ds(0, GROUP - 1)], a2a_send.at[kind, layer])
        return carry

    lax.fori_loop(0, LAYERS, sent, 0)

    @pl.when(away)
    def _():
        land(x_ref, land_x, 0).wait_send()
        land(g_ref, land_g, 1).wait_send()
        remote(hold_x, back_x, back_send.at[0], back_sem.at[0], partner).wait()
        out_x[...] = back_x[...]
        remote(hold_g, back_g, back_send.at[1], back_sem.at[1], partner).wait()
        out_g[...] = back_g[...]

    add_up(0, 0, out_r)


def finish(*refs):
    sources, targets, sem = refs[:4], refs[4:8], refs[8]
    copies = [pltpu.make_async_copy(s, t, sem.at[i]) for i, (s, t) in enumerate(zip(sources, targets))]
    for copy in copies:
        copy.start()
    for copy in copies:
        copy.wait()


def body(inputs, cotangent, right_factor, left_factor):
    vmem = pl.BlockSpec(memory_space=pltpu.VMEM)
    hbm = pl.BlockSpec(memory_space=pl.ANY)
    flat = (ROWS, LANES)
    blocks = (2, 4, 128, 128)
    buffer = lambda n: pltpu.VMEM((n,) + CHUNK, BF)
    dma = pltpu.SemaphoreType.DMA
    outs = pl.pallas_call(
        kernel,
        out_shape=[
            jax.ShapeDtypeStruct(flat, BF),
            jax.ShapeDtypeStruct(flat, BF),
            jax.ShapeDtypeStruct(blocks, F32),
            jax.ShapeDtypeStruct(blocks, F32),
        ],
        in_specs=[vmem, vmem, hbm, hbm],
        out_specs=[vmem] * 4,
        scratch_shapes=[
            pltpu.VMEM((LAYERS, 4, 128, 128), BF), pltpu.VMEM((LAYERS, 4, 128, 128), BF),
            pltpu.VMEM(flat, BF), pltpu.VMEM(flat, BF),
            pltpu.VMEM(flat, BF), pltpu.VMEM(flat, BF),
            pltpu.VMEM(flat, BF), pltpu.VMEM(flat, BF),
            pltpu.VMEM((ROWS, ROWS), BF), pltpu.VMEM((LAYERS, ROWS, ROWS), BF),
            pltpu.VMEM((ROWS, ROWS), BF), pltpu.VMEM((LAYERS, ROWS, ROWS), BF),
            *[pltpu.VMEM((ROWS, ROWS), BF)] * 5,
            buffer(LAYERS + 1), buffer(LAYERS), buffer(LAYERS),
            pltpu.VMEM((LAYERS, 4, 128, LANES), F32),
            buffer(LAYERS), buffer(LAYERS), buffer(LAYERS),
            buffer(LAYERS + 1), buffer(LAYERS), buffer(LAYERS), buffer(LAYERS),
            pltpu.VMEM((2, LAYERS, 4, 128, 128), BF), pltpu.VMEM((2, 2, 4, 4, 128, 128), BF),
            dma((LAYERS,)), dma((LAYERS,)), dma((2, 2, 4)),
            dma((2,)), dma((2,)), dma((2,)), dma((2,)),
            dma((4, LAYERS)), dma((4, LAYERS, 4)), dma((2, LAYERS)), dma((2, 2)),
        ],
        compiler_params=pltpu.CompilerParams(
            collective_id=0, has_side_effects=True, vmem_limit_bytes=56 * 1024 * 1024
        ),
        name="monarch_layers",
    )(
        inputs.reshape(flat),
        cotangent.reshape(flat),
        right_factor.reshape(blocks),
        left_factor.reshape(blocks),
    )
    out_x, out_g, out_r, out_l = pl.pallas_call(
        finish,
        out_shape=[jax.ShapeDtypeStruct(o.shape, o.dtype) for o in outs],
        in_specs=[vmem] * 4,
        out_specs=[hbm] * 4,
        scratch_shapes=[dma((4,))],
        name="finish",
    )(*outs)
    return out_x[None], out_g[None], out_r[:, None], out_l[:, None]


def solution(mesh):
    acts = P("section", "block", None)
    factors = P(None, "section", "block", None, None)
    return jax.shard_map(
        body,
        mesh=mesh,
        in_specs=(acts, acts, factors, factors),
        out_specs=(acts, acts, factors, factors),
        check_vma=False,
    )
```

```python
import functools

import jax
import jax.numpy as jnp
from jax import lax
from jax.experimental import pallas as pl
from jax.experimental.pallas import tpu as pltpu
from jax.sharding import PartitionSpec as P

MESH = pl.DeviceIdType.MESH
BF = jnp.bfloat16
F32 = jnp.float32
GROUP = 32
ROWS = 512
LANES = 128
LAYERS = 8
CHUNK = (GROUP, 16, LANES)


def dot(a, b):
    return jnp.dot(a, b, preferred_element_type=F32)


def sigmoid(v):
    return 0.5 + 0.5 * jnp.tanh(0.5 * v)


def dot_tn(a, b):
    return lax.dot_general(a, b, (((0,), (0,)), ((), ())), preferred_element_type=F32)


def dot_nt(a, b):
    return lax.dot_general(a, b, (((1,), (1,)), ((), ())), preferred_element_type=F32)


def kernel(
    x_ref, g_ref, r_ref, l_ref,
    out_x, out_g, out_r, out_l,
    wr, wl, land_x, land_g, hold_x, hold_g, back_x, back_g,
    rf, rb, lf, lb, m1, px, pxt, pa, pat,
    xs, us, acts, slope, usend, wsend, wrecv, gs, gc, dusend, durecv,
    grads, held,
    wr_sem, wl_sem, w_send, land_sem, land_send, back_sem, back_send,
    a2a_send, a2a_recv, held_send, held_sem,
):
    section = lax.axis_index("section")
    block = lax.axis_index("block")
    yhi, core = section // 2, lax.rem(section, 2)
    xhi, xat, ylo, z = block // 16, lax.rem(block // 8, 2), lax.rem(block // 4, 2), lax.rem(block, 4)
    home = core == xhi
    away = core != xhi
    xlo = lax.rem(xat + xhi + core, 2)
    owned = core * 16 + xlo * 8 + ylo * 4 + z
    place = xlo * 16 + ylo * 8 + core * 4 + z
    micro = 2 * yhi + xhi

    def remote(src, dst, ssem, rsem, device):
        return pltpu.make_async_remote_copy(
            src_ref=src, dst_ref=dst, send_sem=ssem, recv_sem=rsem,
            device_id={"section": device[0], "block": device[1]}, device_id_type=MESH)

    def member(mx, my, mcore, mz):
        at = lax.rem(mx + xhi + mcore, 2)
        return (yhi * 2 + mcore, xhi * 16 + at * 8 + my * 4 + mz)

    partner = (2 * yhi + xhi, owned)

    barrier = pltpu.get_barrier_semaphore()
    greeted = []
    for i in range(1, GROUP):
        greeted.append(member(lax.rem(xlo + i // 16, 2), lax.rem(ylo + (i // 8) % 2, 2),
                              lax.rem(core + (i // 4) % 2, 2), lax.rem(z + i % 4, 4)))
    for dy in range(2):
        for dx in range(2):
            for dc in range(2):
                if dy or dx:
                    greeted.append((2 * lax.rem(yhi + dy, 2) + lax.rem(core + dc, 2),
                                    lax.rem(xhi + dx, 2) * 16 + lax.rem(xat + dx, 2) * 8 + ylo * 4 + z))
    for device in greeted:
        pl.semaphore_signal(barrier, inc=1, device_id={"section": device[0], "block": device[1]},
                            device_id_type=MESH)
    pl.semaphore_wait(barrier, len(greeted))

    def land(src, dst, i):
        return remote(src, dst, land_send.at[i], land_sem.at[i], partner)

    @pl.when(away)
    def _():
        land(x_ref, land_x, 0).start()

    def weight_copies(loop, act, kinds=(0, 1)):
        layer = loop * 4 + section
        for kind in kinds:
            src, dst, sem = ((r_ref, wr, wr_sem), (l_ref, wl, wl_sem))[kind]
            for i in range(4):
                dy, dx = i // 2, i % 2
                to = (2 * lax.rem(yhi + dy, 2) + xhi,
                      lax.rem(xhi + dx, 2) * 16 + lax.rem(xat + dx, 2) * 8 + ylo * 4 + z)
                copy = functools.partial(remote, src.at[loop], dst.at[layer], w_send.at[loop, kind, i],
                                         sem.at[layer], to)
                move = lambda: copy().start() if act == "start" else copy().wait_send()
                if i == 0:
                    @pl.when(home)
                    def _():
                        if act == "start":
                            pltpu.make_async_copy(src.at[loop], dst.at[layer], sem.at[layer]).start()

                    @pl.when(away)
                    def _():
                        move()
                else:
                    move()

    @pl.when(section == 0)
    def _():
        weight_copies(0, "start", (0,))

    def one_hot(of_row, of_column):
        row = lax.broadcasted_iota(jnp.int32, (ROWS, ROWS), 0)
        column = lax.broadcasted_iota(jnp.int32, (ROWS, ROWS), 1)
        return jnp.where(of_row(row) == of_column(column), 1.0, 0.0).astype(BF)

    same = lambda v: v
    quad = lambda v: (((v // 64) % 2) * 16 + (v // 128) * 4 + (v // 16) % 4) * 4
    by_block = lambda v: ((v // 4) % 4) * 128 + quad(v) + v % 4
    by_last = lambda v: (v % 4) * 128 + quad(v) + (v // 4) % 4
    px[...] = one_hot(same, by_block)
    pxt[...] = one_hot(by_block, same)
    pa[...] = one_hot(same, by_last)
    pat[...] = one_hot(by_last, same)

    @pl.when(section != 0)
    def _():
        weight_copies(0, "start", (0,))

    weight_copies(0, "start", (1,))

    @pl.when(away)
    def _():
        land(g_ref, land_g, 1).start()

    def expand(spread, spread_t, weights, forward, backward):
        for b in range(4):
            cols = pl.ds(b * 128, 128)
            m1[:, cols] = dot(spread_t[:, cols], weights[b]).astype(BF)
        for b in range(4):
            rows = pl.ds(b * 128, 128)
            backward[rows, :] = dot(m1[rows, :], spread[...]).astype(BF)
            forward[rows, :] = dot_nt(spread_t[rows, :], m1[...]).astype(BF)

    def wait_bytes(ref, sem):
        pltpu.make_async_copy(ref, ref, sem).wait()

    def expand_right(layer):
        wait_bytes(wr.at[layer], wr_sem.at[layer])
        expand(px, pxt, wr.at[layer], rf, rb.at[layer])

    def expand_left(layer):
        wait_bytes(wl.at[layer], wl_sem.at[layer])
        expand(pa, pat, wl.at[layer], lf, lb.at[layer])

    def chunk_of(relation):
        return lax.rem(xlo + relation // 2, 2) * 2 + lax.rem(ylo + relation % 2, 2)

    def rows_of(ref, chunk):
        return ref.at[pl.ds(chunk * 8, 8)]

    def send_chunk(kind, layer, relation, src, dst):
        chunk = chunk_of(relation)
        for i in (6, 2, 5, 7, 1, 3, 4, 0):
            if relation == 0 and i == 0:
                dst[place] = src[place]
                continue
            mcore, mz = lax.rem(core + i // 4, 2), lax.rem(z + i % 4, 4)
            other = chunk * 8 + mcore * 4 + mz
            remote(src.at[other], dst.at[place], a2a_send.at[kind, layer], a2a_recv.at[kind, layer, relation],
                   member(chunk // 2, lax.rem(chunk, 2), mcore, mz)).start()

    def arrived(kind, layer, relation, dst):
        wait_bytes(dst.at[pl.ds(0, 8 if relation else 7)], a2a_recv.at[kind, layer, relation])

    def stage(arrive, prepare, operand, weights, store, send):
        for relation in range(4):
            arrive(relation)
            if prepare is not None:
                prepare(chunk_of(relation))
        value = operand[...].reshape(ROWS, LANES)
        for pair in ((3, 2), (1, 0)):
            for relation in pair:
                chunk = chunk_of(relation)
                rows = pl.ds(pl.multiple_of(chunk * 128, 128), 128)
                store(chunk, dot(weights[rows, :], value))
            for relation in pair:
                send(relation)

    def to_owner(kind, layer, src, act):
        loop, owner = layer // 4, lax.rem(layer, 4)
        mine = (owner == section) & home
        other = (owner != section) | away
        dst = held.at[loop, kind, micro]

        @pl.when(mine)
        def _():
            if act == "start":
                pltpu.make_async_copy(src, dst, held_sem.at[loop, kind]).start()

        @pl.when(other)
        def _():
            copy = remote(src, dst, held_send.at[kind, layer], held_sem.at[loop, kind], (owner, owned))
            if act == "start":
                copy.start()
            else:
                copy.wait_send()

    def flat(ref, chunk):
        return rows_of(ref, chunk)[...].reshape(128, LANES)

    def put(ref, chunk, value):
        rows_of(ref, chunk)[...] = value.reshape(8, 16, LANES)

    @pl.when(away)
    def _():
        wait_bytes(land_x, land_sem.at[0])
        hold_x[...] = land_x[...]

    @pl.when(home)
    def _():
        hold_x[...] = x_ref[...]

    xs[0] = dot(pxt[...], hold_x[...]).astype(BF).reshape(CHUNK)
    wait_bytes(wr.at[0], wr_sem.at[0])
    for b in range(4):
        rows = pl.ds(b * 128, 128)
        hold_g[rows, :] = dot_tn(wr[0, b], hold_x[rows, :]).astype(BF)
    stage(
        lambda relation: None,
        None,
        hold_g,
        pxt,
        lambda chunk, value: put(usend.at[0], chunk, value.astype(BF)),
        lambda relation: send_chunk(0, 0, relation, usend.at[0], us.at[0]),
    )
    weight_copies(1, "start", (0,))
    expand_left(0)

    @pl.when(away)
    def _():
        wait_bytes(land_g, land_sem.at[1])
        gs[LAYERS] = dot(pxt[...], land_g[...]).astype(BF).reshape(CHUNK)

    @pl.when(home)
    def _():
        gs[LAYERS] = dot(pxt[...], g_ref[...]).astype(BF).reshape(CHUNK)

    for relation in (3, 2, 1, 0):
        send_chunk(2, LAYERS - 1, relation, gs.at[LAYERS], gc.at[LAYERS - 1])

    def forward_layer(layer, carry):
        def activate(chunk):
            v = flat(us.at[layer], chunk).astype(F32)
            put(acts.at[layer], chunk, (v * sigmoid(v)).astype(BF))

        stage(
            lambda relation: arrived(0, layer, relation, us.at[layer]),
            activate,
            acts.at[layer],
            lf,
            lambda chunk, value: put(wsend.at[layer], chunk, value.astype(BF)),
            lambda relation: send_chunk(1, layer, relation, wsend.at[layer], wrecv.at[layer]),
        )

        @pl.when(layer == 0)
        def _():
            weight_copies(1, "start", (1,))

        for chunk in range(4):
            v = flat(us.at[layer], chunk).astype(F32)
            gate = sigmoid(v)
            slope[layer, chunk] = gate * (1.0 + v * (1.0 - gate))

        def step(chunk):
            new = flat(xs.at[layer], chunk).astype(F32) + flat(wrecv.at[layer], chunk).astype(F32)
            put(xs.at[layer + 1], chunk, new.astype(BF))

        expand_right(layer + 1)
        stage(
            lambda relation: arrived(1, layer, relation, wrecv.at[layer]),
            step,
            xs.at[layer + 1],
            rf,
            lambda chunk, value: put(usend.at[layer + 1], chunk, value.astype(BF)),
            lambda relation: send_chunk(0, layer + 1, relation, usend.at[layer + 1], us.at[layer + 1]),
        )
        expand_left(layer + 1)
        return carry

    lax.fori_loop(0, LAYERS - 1, forward_layer, 0)

    def give_back(i, src, dst, local):
        @pl.when(away)
        def _():
            remote(src, dst, back_send.at[i], back_sem.at[i], partner).start()

        @pl.when(home)
        def _():
            local[...] = src[...]


    def weight_grad(kind, layer, spread, left, right):
        a = dot(spread[...], left[layer].reshape(ROWS, LANES)).astype(BF)
        b = dot(spread[...], right[layer].reshape(ROWS, LANES)).astype(BF)
        for i in range(4):
            rows = slice(i * 128, i * 128 + 128)
            grads[kind, layer, i] = dot_nt(a[rows], b[rows]).astype(BF)
        to_owner(kind, layer, grads.at[kind, layer], "start")

    def add_up(loop, kind, out):
        wait_bytes(held.at[loop, kind], held_sem.at[loop, kind])
        for i in range(4):
            terms = [held[loop, kind, m, i].astype(F32) for m in range(4)]
            out[loop, i] = (terms[0] + terms[1]) + (terms[2] + terms[3])

    def backward_layer(step, carry):
        layer = LAYERS - 1 - step

        def send_back(relation):
            @pl.when(layer > 0)
            def _():
                send_chunk(2, layer - 1, relation, gs.at[layer], gc.at[layer - 1])

        stage(
            lambda relation: arrived(2, layer, relation, gc.at[layer]),
            None,
            gc.at[layer],
            lb.at[layer],
            lambda chunk, value: put(dusend.at[layer], chunk, (value * slope[layer, chunk]).astype(BF)),
            lambda relation: send_chunk(3, layer, relation, dusend.at[layer], durecv.at[layer]),
        )
        weight_grad(1, layer, pa, acts, gc)

        @pl.when(step == 5)
        def _():
            add_up(1, 0, out_r)

        @pl.when(step == 6)
        def _():
            add_up(1, 1, out_l)

        for relation in range(4):
            arrived(3, layer, relation, durecv.at[layer])

        @pl.when(layer == 0)
        def _():
            weight_grad(0, layer, px, xs, durecv)

        stage(
            lambda relation: None,
            None,
            durecv.at[layer],
            rb.at[layer],
            lambda chunk, value: put(
                gs.at[layer], chunk, (flat(gs.at[layer + 1], chunk).astype(F32) + value).astype(BF)),
            send_back,
        )

        @pl.when(layer > 0)
        def _():
            weight_grad(0, layer, px, xs, durecv)

        return carry

    top = LAYERS - 1
    for relation in range(4):
        arrived(2, top, relation, gc.at[top])
    d_act = dot(lb[top], gc[top].reshape(ROWS, LANES))
    for chunk in range(4):
        slope[top, chunk] = d_act[chunk * 128 : chunk * 128 + 128]
    for relation in range(4):
        arrived(0, top, relation, us.at[top])
    for chunk in range(4):
        v = flat(us.at[top], chunk).astype(F32)
        gate = sigmoid(v)
        put(dusend.at[top], chunk, (slope[top, chunk] * (gate * (1.0 + v * (1.0 - gate)))).astype(BF))
        put(acts.at[top], chunk, (v * gate).astype(BF))
    for relation in (3, 2, 1, 0):
        send_chunk(3, top, relation, dusend.at[top], durecv.at[top])
    stage(
        lambda relation: None,
        None,
        acts.at[top],
        lf,
        lambda chunk, value: put(wsend.at[top], chunk, value.astype(BF)),
        lambda relation: send_chunk(1, top, relation, wsend.at[top], wrecv.at[top]),
    )
    weight_grad(1, top, pa, acts, gc)
    expand(px, pxt, wr.at[0], rf, rb.at[0])
    stage(
        lambda relation: arrived(3, top, relation, durecv.at[top]),
        None,
        durecv.at[top],
        rb.at[top],
        lambda chunk, value: put(
            gs.at[top], chunk, (flat(gs.at[LAYERS], chunk).astype(F32) + value).astype(BF)),
        lambda relation: send_chunk(2, top - 1, relation, gs.at[top], gc.at[top - 1]),
    )
    weight_grad(0, top, px, xs, durecv)
    for relation in range(4):
        arrived(1, top, relation, wrecv.at[top])
    last = xs[top].astype(F32) + wrecv[top].astype(F32)
    hold_x[...] = dot(px[...], last.astype(BF).reshape(ROWS, LANES)).astype(BF)
    give_back(0, hold_x, back_x, out_x)

    lax.fori_loop(1, LAYERS, backward_layer, 0)

    hold_g[...] = dot(px[...], gs[0].reshape(ROWS, LANES)).astype(BF)
    give_back(1, hold_g, back_g, out_g)
    add_up(0, 1, out_l)

    weight_copies(0, "wait")
    weight_copies(1, "wait")

    def sent(layer, carry):
        for kind in range(2):
            to_owner(kind, layer, grads.at[kind, layer], "wait")
        for kind in range(4):
            wait_bytes(usend.at[layer, pl.ds(0, GROUP - 1)], a2a_send.at[kind, layer])
        return carry

    lax.fori_loop(0, LAYERS, sent, 0)

    @pl.when(away)
    def _():
        land(x_ref, land_x, 0).wait_send()
        land(g_ref, land_g, 1).wait_send()
        remote(hold_x, back_x, back_send.at[0], back_sem.at[0], partner).wait()
        out_x[...] = back_x[...]
        remote(hold_g, back_g, back_send.at[1], back_sem.at[1], partner).wait()
        out_g[...] = back_g[...]

    add_up(0, 0, out_r)


def finish(*refs):
    sources, targets, sem = refs[:4], refs[4:8], refs[8]
    copies = [pltpu.make_async_copy(s, t, sem.at[i]) for i, (s, t) in enumerate(zip(sources, targets))]
    for copy in copies:
        copy.start()
    for copy in copies:
        copy.wait()


def body(inputs, cotangent, right_factor, left_factor):
    vmem = pl.BlockSpec(memory_space=pltpu.VMEM)
    hbm = pl.BlockSpec(memory_space=pl.ANY)
    flat = (ROWS, LANES)
    blocks = (2, 4, 128, 128)
    buffer = lambda n: pltpu.VMEM((n,) + CHUNK, BF)
    dma = pltpu.SemaphoreType.DMA
    outs = pl.pallas_call(
        kernel,
        out_shape=[
            jax.ShapeDtypeStruct(flat, BF),
            jax.ShapeDtypeStruct(flat, BF),
            jax.ShapeDtypeStruct(blocks, F32),
            jax.ShapeDtypeStruct(blocks, F32),
        ],
        in_specs=[vmem, vmem, hbm, hbm],
        out_specs=[vmem] * 4,
        scratch_shapes=[
            pltpu.VMEM((LAYERS, 4, 128, 128), BF), pltpu.VMEM((LAYERS, 4, 128, 128), BF),
            pltpu.VMEM(flat, BF), pltpu.VMEM(flat, BF),
            pltpu.VMEM(flat, BF), pltpu.VMEM(flat, BF),
            pltpu.VMEM(flat, BF), pltpu.VMEM(flat, BF),
            pltpu.VMEM((ROWS, ROWS), BF), pltpu.VMEM((LAYERS, ROWS, ROWS), BF),
            pltpu.VMEM((ROWS, ROWS), BF), pltpu.VMEM((LAYERS, ROWS, ROWS), BF),
            *[pltpu.VMEM((ROWS, ROWS), BF)] * 5,
            buffer(LAYERS), buffer(LAYERS), buffer(LAYERS),
            pltpu.VMEM((LAYERS, 4, 128, LANES), F32),
            buffer(LAYERS), buffer(LAYERS), buffer(LAYERS),
            buffer(LAYERS + 1), buffer(LAYERS), buffer(LAYERS), buffer(LAYERS),
            pltpu.VMEM((2, LAYERS, 4, 128, 128), BF), pltpu.VMEM((2, 2, 4, 4, 128, 128), BF),
            dma((LAYERS,)), dma((LAYERS,)), dma((2, 2, 4)),
            dma((2,)), dma((2,)), dma((2,)), dma((2,)),
            dma((4, LAYERS)), dma((4, LAYERS, 4)), dma((2, LAYERS)), dma((2, 2)),
        ],
        compiler_params=pltpu.CompilerParams(
            collective_id=0, has_side_effects=True, vmem_limit_bytes=56 * 1024 * 1024
        ),
        name="monarch_layers",
    )(
        inputs.reshape(flat),
        cotangent.reshape(flat),
        right_factor.reshape(blocks),
        left_factor.reshape(blocks),
    )
    out_x, out_g, out_r, out_l = pl.pallas_call(
        finish,
        out_shape=[jax.ShapeDtypeStruct(o.shape, o.dtype) for o in outs],
        in_specs=[vmem] * 4,
        out_specs=[hbm] * 4,
        scratch_shapes=[dma((4,))],
        name="finish",
    )(*outs)
    return out_x[None], out_g[None], out_r[:, None], out_l[:, None]


def solution(mesh):
    acts = P("section", "block", None)
    factors = P(None, "section", "block", None, None)
    return jax.shard_map(
        body,
        mesh=mesh,
        in_specs=(acts, acts, factors, factors),
        out_specs=(acts, acts, factors, factors),
        check_vma=False,
    )
```

```python
import functools

import jax
import jax.numpy as jnp
from jax import lax
from jax.experimental import pallas as pl
from jax.experimental.pallas import tpu as pltpu
from jax.sharding import PartitionSpec as P

MESH = pl.DeviceIdType.MESH
BF = jnp.bfloat16
F32 = jnp.float32
GROUP = 32
ROWS = 512
LANES = 128
LAYERS = 8
CHUNK = (GROUP, 16, LANES)


def dot(a, b):
    return jnp.dot(a, b, preferred_element_type=F32)


def sigmoid(v):
    return 0.5 + 0.5 * jnp.tanh(0.5 * v)


def dot_tn(a, b):
    return lax.dot_general(a, b, (((0,), (0,)), ((), ())), preferred_element_type=F32)


def dot_nt(a, b):
    return lax.dot_general(a, b, (((1,), (1,)), ((), ())), preferred_element_type=F32)


def kernel(
    x_ref, g_ref, r_ref, l_ref,
    out_x, out_g, out_r, out_l,
    wr, wl, land_x, land_g, hold_x, hold_g, back_x, back_g,
    rf, rb, lf, lb, m1, px, pxt, pa, pat,
    xs, us, acts, slope, usend, wsend, wrecv, gs, gc, dusend, durecv,
    grads, held,
    wr_sem, wl_sem, w_send, land_sem, land_send, back_sem, back_send,
    a2a_send, a2a_recv, held_send, held_sem,
):
    section = lax.axis_index("section")
    block = lax.axis_index("block")
    yhi, core = section // 2, lax.rem(section, 2)
    xhi, xat, ylo, z = block // 16, lax.rem(block // 8, 2), lax.rem(block // 4, 2), lax.rem(block, 4)
    home = core == xhi
    away = core != xhi
    xlo = lax.rem(xat + xhi + core, 2)
    owned = core * 16 + xlo * 8 + ylo * 4 + z
    place = xlo * 16 + ylo * 8 + core * 4 + z
    micro = 2 * yhi + xhi

    def remote(src, dst, ssem, rsem, device):
        return pltpu.make_async_remote_copy(
            src_ref=src, dst_ref=dst, send_sem=ssem, recv_sem=rsem,
            device_id={"section": device[0], "block": device[1]}, device_id_type=MESH)

    def member(mx, my, mcore, mz):
        at = lax.rem(mx + xhi + mcore, 2)
        return (yhi * 2 + mcore, xhi * 16 + at * 8 + my * 4 + mz)

    partner = (2 * yhi + xhi, owned)

    barrier = pltpu.get_barrier_semaphore()
    greeted = []
    for i in range(1, GROUP):
        greeted.append(member(lax.rem(xlo + i // 16, 2), lax.rem(ylo + (i // 8) % 2, 2),
                              lax.rem(core + (i // 4) % 2, 2), lax.rem(z + i % 4, 4)))
    for dy in range(2):
        for dx in range(2):
            for dc in range(2):
                if dy or dx:
                    greeted.append((2 * lax.rem(yhi + dy, 2) + lax.rem(core + dc, 2),
                                    lax.rem(xhi + dx, 2) * 16 + lax.rem(xat + dx, 2) * 8 + ylo * 4 + z))
    for device in greeted:
        pl.semaphore_signal(barrier, inc=1, device_id={"section": device[0], "block": device[1]},
                            device_id_type=MESH)
    pl.semaphore_wait(barrier, len(greeted))

    def land(src, dst, i):
        return remote(src, dst, land_send.at[i], land_sem.at[i], partner)

    @pl.when(away)
    def _():
        land(x_ref, land_x, 0).start()

    def weight_copies(loop, act, kinds=(0, 1)):
        layer = loop * 4 + section
        for kind in kinds:
            src, dst, sem = ((r_ref, wr, wr_sem), (l_ref, wl, wl_sem))[kind]
            for i in range(4):
                dy, dx = i // 2, i % 2
                to = (2 * lax.rem(yhi + dy, 2) + xhi,
                      lax.rem(xhi + dx, 2) * 16 + lax.rem(xat + dx, 2) * 8 + ylo * 4 + z)
                copy = functools.partial(remote, src.at[loop], dst.at[layer], w_send.at[loop, kind, i],
                                         sem.at[layer], to)
                move = lambda: copy().start() if act == "start" else copy().wait_send()
                if i == 0:
                    @pl.when(home)
                    def _():
                        if act == "start":
                            pltpu.make_async_copy(src.at[loop], dst.at[layer], sem.at[layer]).start()

                    @pl.when(away)
                    def _():
                        move()
                else:
                    move()

    @pl.when(section == 0)
    def _():
        weight_copies(0, "start", (0,))

    def one_hot(of_row, of_column):
        row = lax.broadcasted_iota(jnp.int32, (ROWS, ROWS), 0)
        column = lax.broadcasted_iota(jnp.int32, (ROWS, ROWS), 1)
        return jnp.where(of_row(row) == of_column(column), 1.0, 0.0).astype(BF)

    same = lambda v: v
    quad = lambda v: (((v // 64) % 2) * 16 + (v // 128) * 4 + (v // 16) % 4) * 4
    by_block = lambda v: ((v // 4) % 4) * 128 + quad(v) + v % 4
    by_last = lambda v: (v % 4) * 128 + quad(v) + (v // 4) % 4
    px[...] = one_hot(same, by_block)
    pxt[...] = one_hot(by_block, same)
    pa[...] = one_hot(same, by_last)
    pat[...] = one_hot(by_last, same)

    @pl.when(section != 0)
    def _():
        weight_copies(0, "start", (0,))

    @pl.when(section == 0)
    def _():
        weight_copies(0, "start", (1,))

    @pl.when(away)
    def _():
        land(g_ref, land_g, 1).start()

    def expand(spread, spread_t, weights, forward, backward):
        for b in range(4):
            cols = pl.ds(b * 128, 128)
            m1[:, cols] = dot(spread_t[:, cols], weights[b]).astype(BF)
        for b in range(4):
            rows = pl.ds(b * 128, 128)
            backward[rows, :] = dot(m1[rows, :], spread[...]).astype(BF)
            forward[rows, :] = dot_nt(spread_t[rows, :], m1[...]).astype(BF)

    def wait_bytes(ref, sem):
        pltpu.make_async_copy(ref, ref, sem).wait()

    def expand_right(layer):
        wait_bytes(wr.at[layer], wr_sem.at[layer])
        expand(px, pxt, wr.at[layer], rf, rb.at[layer])

    def expand_left(layer):
        wait_bytes(wl.at[layer], wl_sem.at[layer])
        expand(pa, pat, wl.at[layer], lf, lb.at[layer])

    def chunk_of(relation):
        return lax.rem(xlo + relation // 2, 2) * 2 + lax.rem(ylo + relation % 2, 2)

    def rows_of(ref, chunk):
        return ref.at[pl.ds(chunk * 8, 8)]

    def send_chunk(kind, layer, relation, src, dst):
        chunk = chunk_of(relation)
        for i in (6, 2, 5, 7, 1, 3, 4, 0):
            if relation == 0 and i == 0:
                dst[place] = src[place]
                continue
            mcore, mz = lax.rem(core + i // 4, 2), lax.rem(z + i % 4, 4)
            other = chunk * 8 + mcore * 4 + mz
            remote(src.at[other], dst.at[place], a2a_send.at[kind, layer], a2a_recv.at[kind, layer, relation],
                   member(chunk // 2, lax.rem(chunk, 2), mcore, mz)).start()

    def arrived(kind, layer, relation, dst):
        wait_bytes(dst.at[pl.ds(0, 8 if relation else 7)], a2a_recv.at[kind, layer, relation])

    def stage(arrive, prepare, operand, weights, store, send):
        for relation in range(4):
            arrive(relation)
            if prepare is not None:
                prepare(chunk_of(relation))
        value = operand[...].reshape(ROWS, LANES)
        for pair in ((3, 2), (1, 0)):
            for relation in pair:
                chunk = chunk_of(relation)
                rows = pl.ds(pl.multiple_of(chunk * 128, 128), 128)
                store(chunk, dot(weights[rows, :], value))
            for relation in pair:
                send(relation)

    def to_owner(kind, layer, src, act):
        loop, owner = layer // 4, lax.rem(layer, 4)
        mine = (owner == section) & home
        other = (owner != section) | away
        dst = held.at[loop, kind, micro]

        @pl.when(mine)
        def _():
            if act == "start":
                pltpu.make_async_copy(src, dst, held_sem.at[loop, kind]).start()

        @pl.when(other)
        def _():
            copy = remote(src, dst, held_send.at[kind, layer], held_sem.at[loop, kind], (owner, owned))
            if act == "start":
                copy.start()
            else:
                copy.wait_send()

    def flat(ref, chunk):
        return rows_of(ref, chunk)[...].reshape(128, LANES)

    def put(ref, chunk, value):
        rows_of(ref, chunk)[...] = value.reshape(8, 16, LANES)

    @pl.when(away)
    def _():
        wait_bytes(land_x, land_sem.at[0])
        hold_x[...] = land_x[...]

    @pl.when(home)
    def _():
        hold_x[...] = x_ref[...]

    xs[0] = dot(pxt[...], hold_x[...]).astype(BF).reshape(CHUNK)
    wait_bytes(wr.at[0], wr_sem.at[0])
    for b in range(4):
        rows = pl.ds(b * 128, 128)
        hold_g[rows, :] = dot_tn(wr[0, b], hold_x[rows, :]).astype(BF)
    stage(
        lambda relation: None,
        None,
        hold_g,
        pxt,
        lambda chunk, value: put(usend.at[0], chunk, value.astype(BF)),
        lambda relation: send_chunk(0, 0, relation, usend.at[0], us.at[0]),
    )

    @pl.when(section != 0)
    def _():
        weight_copies(0, "start", (1,))

    expand_left(0)

    @pl.when(away)
    def _():
        wait_bytes(land_g, land_sem.at[1])
        gs[LAYERS] = dot(pxt[...], land_g[...]).astype(BF).reshape(CHUNK)

    @pl.when(home)
    def _():
        gs[LAYERS] = dot(pxt[...], g_ref[...]).astype(BF).reshape(CHUNK)

    for relation in (3, 2, 1, 0):
        send_chunk(2, LAYERS - 1, relation, gs.at[LAYERS], gc.at[LAYERS - 1])

    def forward_layer(layer, carry):
        def activate(chunk):
            v = flat(us.at[layer], chunk).astype(F32)
            put(acts.at[layer], chunk, (v * sigmoid(v)).astype(BF))

        stage(
            lambda relation: arrived(0, layer, relation, us.at[layer]),
            activate,
            acts.at[layer],
            lf,
            lambda chunk, value: put(wsend.at[layer], chunk, value.astype(BF)),
            lambda relation: send_chunk(1, layer, relation, wsend.at[layer], wrecv.at[layer]),
        )

        @pl.when(layer == 1)
        def _():
            weight_copies(1, "start", (0,))

        @pl.when(layer == 2)
        def _():
            weight_copies(1, "start", (1,))

        for chunk in range(4):
            v = flat(us.at[layer], chunk).astype(F32)
            gate = sigmoid(v)
            slope[layer, chunk] = gate * (1.0 + v * (1.0 - gate))

        def step(chunk):
            new = flat(xs.at[layer], chunk).astype(F32) + flat(wrecv.at[layer], chunk).astype(F32)
            put(xs.at[layer + 1], chunk, new.astype(BF))

        expand_right(layer + 1)
        stage(
            lambda relation: arrived(1, layer, relation, wrecv.at[layer]),
            step,
            xs.at[layer + 1],
            rf,
            lambda chunk, value: put(usend.at[layer + 1], chunk, value.astype(BF)),
            lambda relation: send_chunk(0, layer + 1, relation, usend.at[layer + 1], us.at[layer + 1]),
        )
        expand_left(layer + 1)
        return carry

    lax.fori_loop(0, LAYERS - 1, forward_layer, 0)

    def give_back(i, src, dst, local):
        @pl.when(away)
        def _():
            remote(src, dst, back_send.at[i], back_sem.at[i], partner).start()

        @pl.when(home)
        def _():
            local[...] = src[...]


    def weight_grad(kind, layer, spread, left, right):
        a = dot(spread[...], left[layer].reshape(ROWS, LANES)).astype(BF)
        b = dot(spread[...], right[layer].reshape(ROWS, LANES)).astype(BF)
        for i in range(4):
            rows = slice(i * 128, i * 128 + 128)
            grads[kind, layer, i] = dot_nt(a[rows], b[rows]).astype(BF)
        to_owner(kind, layer, grads.at[kind, layer], "start")

    def add_up(loop, kind, out):
        wait_bytes(held.at[loop, kind], held_sem.at[loop, kind])
        for i in range(4):
            terms = [held[loop, kind, m, i].astype(F32) for m in range(4)]
            out[loop, i] = (terms[0] + terms[1]) + (terms[2] + terms[3])

    def backward_layer(step, carry):
        layer = LAYERS - 1 - step

        def send_back(relation):
            @pl.when(layer > 0)
            def _():
                send_chunk(2, layer - 1, relation, gs.at[layer], gc.at[layer - 1])

        stage(
            lambda relation: arrived(2, layer, relation, gc.at[layer]),
            None,
            gc.at[layer],
            lb.at[layer],
            lambda chunk, value: put(dusend.at[layer], chunk, (value * slope[layer, chunk]).astype(BF)),
            lambda relation: send_chunk(3, layer, relation, dusend.at[layer], durecv.at[layer]),
        )
        weight_grad(1, layer, pa, acts, gc)

        @pl.when(step == 5)
        def _():
            add_up(1, 0, out_r)

        @pl.when(step == 6)
        def _():
            add_up(1, 1, out_l)

        for relation in range(4):
            arrived(3, layer, relation, durecv.at[layer])

        @pl.when(layer == 0)
        def _():
            weight_grad(0, layer, px, xs, durecv)

        stage(
            lambda relation: None,
            None,
            durecv.at[layer],
            rb.at[layer],
            lambda chunk, value: put(
                gs.at[layer], chunk, (flat(gs.at[layer + 1], chunk).astype(F32) + value).astype(BF)),
            send_back,
        )

        @pl.when(layer > 0)
        def _():
            weight_grad(0, layer, px, xs, durecv)

        return carry

    top = LAYERS - 1
    for relation in range(4):
        arrived(2, top, relation, gc.at[top])
    d_act = dot(lb[top], gc[top].reshape(ROWS, LANES))
    for chunk in range(4):
        slope[top, chunk] = d_act[chunk * 128 : chunk * 128 + 128]
    for relation in range(4):
        arrived(0, top, relation, us.at[top])
    for chunk in range(4):
        v = flat(us.at[top], chunk).astype(F32)
        gate = sigmoid(v)
        put(dusend.at[top], chunk, (slope[top, chunk] * (gate * (1.0 + v * (1.0 - gate)))).astype(BF))
        put(acts.at[top], chunk, (v * gate).astype(BF))
    for relation in (3, 2, 1, 0):
        send_chunk(3, top, relation, dusend.at[top], durecv.at[top])
    stage(
        lambda relation: None,
        None,
        acts.at[top],
        lf,
        lambda chunk, value: put(wsend.at[top], chunk, value.astype(BF)),
        lambda relation: send_chunk(1, top, relation, wsend.at[top], wrecv.at[top]),
    )
    weight_grad(1, top, pa, acts, gc)
    expand(px, pxt, wr.at[0], rf, rb.at[0])
    stage(
        lambda relation: arrived(3, top, relation, durecv.at[top]),
        None,
        durecv.at[top],
        rb.at[top],
        lambda chunk, value: put(
            gs.at[top], chunk, (flat(gs.at[LAYERS], chunk).astype(F32) + value).astype(BF)),
        lambda relation: send_chunk(2, top - 1, relation, gs.at[top], gc.at[top - 1]),
    )
    weight_grad(0, top, px, xs, durecv)
    for relation in range(4):
        arrived(1, top, relation, wrecv.at[top])
    last = xs[top].astype(F32) + wrecv[top].astype(F32)
    hold_x[...] = dot(px[...], last.astype(BF).reshape(ROWS, LANES)).astype(BF)
    give_back(0, hold_x, back_x, out_x)

    lax.fori_loop(1, LAYERS, backward_layer, 0)

    hold_g[...] = dot(px[...], gs[0].reshape(ROWS, LANES)).astype(BF)
    give_back(1, hold_g, back_g, out_g)
    add_up(0, 1, out_l)

    weight_copies(0, "wait")
    weight_copies(1, "wait")

    def sent(layer, carry):
        for kind in range(2):
            to_owner(kind, layer, grads.at[kind, layer], "wait")
        for kind in range(4):
            wait_bytes(usend.at[layer, pl.ds(0, GROUP - 1)], a2a_send.at[kind, layer])
        return carry

    lax.fori_loop(0, LAYERS, sent, 0)

    @pl.when(away)
    def _():
        land(x_ref, land_x, 0).wait_send()
        land(g_ref, land_g, 1).wait_send()
        remote(hold_x, back_x, back_send.at[0], back_sem.at[0], partner).wait()
        out_x[...] = back_x[...]
        remote(hold_g, back_g, back_send.at[1], back_sem.at[1], partner).wait()
        out_g[...] = back_g[...]

    add_up(0, 0, out_r)


def finish(*refs):
    sources, targets, sem = refs[:4], refs[4:8], refs[8]
    copies = [pltpu.make_async_copy(s, t, sem.at[i]) for i, (s, t) in enumerate(zip(sources, targets))]
    for copy in copies:
        copy.start()
    for copy in copies:
        copy.wait()


def body(inputs, cotangent, right_factor, left_factor):
    vmem = pl.BlockSpec(memory_space=pltpu.VMEM)
    hbm = pl.BlockSpec(memory_space=pl.ANY)
    flat = (ROWS, LANES)
    blocks = (2, 4, 128, 128)
    buffer = lambda n: pltpu.VMEM((n,) + CHUNK, BF)
    dma = pltpu.SemaphoreType.DMA
    outs = pl.pallas_call(
        kernel,
        out_shape=[
            jax.ShapeDtypeStruct(flat, BF),
            jax.ShapeDtypeStruct(flat, BF),
            jax.ShapeDtypeStruct(blocks, F32),
            jax.ShapeDtypeStruct(blocks, F32),
        ],
        in_specs=[vmem, vmem, hbm, hbm],
        out_specs=[vmem] * 4,
        scratch_shapes=[
            pltpu.VMEM((LAYERS, 4, 128, 128), BF), pltpu.VMEM((LAYERS, 4, 128, 128), BF),
            pltpu.VMEM(flat, BF), pltpu.VMEM(flat, BF),
            pltpu.VMEM(flat, BF), pltpu.VMEM(flat, BF),
            pltpu.VMEM(flat, BF), pltpu.VMEM(flat, BF),
            pltpu.VMEM((ROWS, ROWS), BF), pltpu.VMEM((LAYERS, ROWS, ROWS), BF),
            pltpu.VMEM((ROWS, ROWS), BF), pltpu.VMEM((LAYERS, ROWS, ROWS), BF),
            *[pltpu.VMEM((ROWS, ROWS), BF)] * 5,
            buffer(LAYERS), buffer(LAYERS), buffer(LAYERS),
            pltpu.VMEM((LAYERS, 4, 128, LANES), F32),
            buffer(LAYERS), buffer(LAYERS), buffer(LAYERS),
            buffer(LAYERS + 1), buffer(LAYERS), buffer(LAYERS), buffer(LAYERS),
            pltpu.VMEM((2, LAYERS, 4, 128, 128), BF), pltpu.VMEM((2, 2, 4, 4, 128, 128), BF),
            dma((LAYERS,)), dma((LAYERS,)), dma((2, 2, 4)),
            dma((2,)), dma((2,)), dma((2,)), dma((2,)),
            dma((4, LAYERS)), dma((4, LAYERS, 4)), dma((2, LAYERS)), dma((2, 2)),
        ],
        compiler_params=pltpu.CompilerParams(
            collective_id=0, has_side_effects=True, vmem_limit_bytes=56 * 1024 * 1024
        ),
        name="monarch_layers",
    )(
        inputs.reshape(flat),
        cotangent.reshape(flat),
        right_factor.reshape(blocks),
        left_factor.reshape(blocks),
    )
    out_x, out_g, out_r, out_l = pl.pallas_call(
        finish,
        out_shape=[jax.ShapeDtypeStruct(o.shape, o.dtype) for o in outs],
        in_specs=[vmem] * 4,
        out_specs=[hbm] * 4,
        scratch_shapes=[dma((4,))],
        name="finish",
    )(*outs)
    return out_x[None], out_g[None], out_r[:, None], out_l[:, None]


def solution(mesh):
    acts = P("section", "block", None)
    factors = P(None, "section", "block", None, None)
    return jax.shard_map(
        body,
        mesh=mesh,
        in_specs=(acts, acts, factors, factors),
        out_specs=(acts, acts, factors, factors),
        check_vma=False,
    )
```
